32 devices in a mesh: fsdp: 4 (over z), ctx: 2 (over x), tp: 4 (over y, core).
Axes of the slice: x: 2, y: 2, z: 4, core: 2. Of those that a mesh axis runs over, the one named last changes fastest.
Arguments:
- mel_frames: bfloat16 [16, 2048, 80], P('fsdp', 'ctx'), may hold values from -6 to 6
- dec_ids: int32 [16, 512], P('fsdp', 'ctx'), may hold values from 0 to 51871
- targets: int32 [16, 512], P('fsdp', 'ctx'), may hold values from 0 to 51871
- teach_rows: int32 [16, 128], P('fsdp', 'ctx'), may hold values from 0 to 511, as said below
- teach_ids: int32 [16, 128, 64], P('fsdp', 'ctx'), may hold values from 0 to 51871
- teach_probs: float32 [16, 128, 64], P('fsdp', 'ctx'), may hold values from 0.002 to 0.03
- vocab_mask: int32 [51872], P('tp'), may hold values 0 or 1
- projections: float32 [9, 768, 768], P(None, ('fsdp', 'ctx'), 'tp'), may hold values from -0.21875 to 0.21875
- out_proj: float32 [3, 768, 768], P(None, ('fsdp', 'ctx'), 'tp'), may hold values from -0.875 to 0.875
- feed_forward: float32 [4, 768, 3072], P(None, ('fsdp', 'ctx'), 'tp'), may hold values from -0.21875 to 0.21875
- conv_kernels: float32 [2304, 768], P(('fsdp', 'ctx'), 'tp'), may hold values from -0.125 to 0.125
- embed_table: float32 [51872, 768], P('tp', ('fsdp', 'ctx')), may hold values from -0.625 to 0.625
- small_params: float32 [787, 768], replicated, may hold values from -2 to 2
- moment_projections: float32 [9, 768, 768], P(None, ('fsdp', 'ctx'), 'tp'), may hold values from -0.00061035156 to 0.00061035156
- moment_out_proj: float32 [3, 768, 768], P(None, ('fsdp', 'ctx'), 'tp'), may hold values from -0.00061035156 to 0.00061035156
- moment_feed_forward: float32 [4, 768, 3072], P(None, ('fsdp', 'ctx'), 'tp'), may hold values from -0.00061035156 to 0.00061035156
- moment_conv_kernels: float32 [2304, 768], P(('fsdp', 'ctx'), 'tp'), may hold values from -0.00061035156 to 0.00061035156
- moment_embed_table: float32 [51872, 768], P('tp', ('fsdp', 'ctx')), may hold values from -0.00061035156 to 0.00061035156
- moment_small_params: float32 [787, 768], replicated, may hold values from -0.00061035156 to 0.00061035156
- average_projections: float32 [9, 768, 768], P(None, ('fsdp', 'ctx'), 'tp'), may hold values from -0.21875 to 0.21875
- average_out_proj: float32 [3, 768, 768], P(None, ('fsdp', 'ctx'), 'tp'), may hold values from -0.875 to 0.875
- average_feed_forward: float32 [4, 768, 3072], P(None, ('fsdp', 'ctx'), 'tp'), may hold values from -0.21875 to 0.21875
- average_conv_kernels: float32 [2304, 768], P(('fsdp', 'ctx'), 'tp'), may hold values from -0.125 to 0.125
- average_embed_table: float32 [51872, 768], P('tp', ('fsdp', 'ctx')), may hold values from -0.625 to 0.625
- average_small_params: float32 [787, 768], replicated, may hold values from -2 to 2
Outputs:
- loss: float32 [], replicated
- grad_norm: float32 [], replicated
- update_projections: float32 [9, 768, 768], P(None, ('fsdp', 'ctx'), 'tp')
- update_out_proj: float32 [3, 768, 768], P(None, ('fsdp', 'ctx'), 'tp')
- update_feed_forward: float32 [4, 768, 3072], P(None, ('fsdp', 'ctx'), 'tp')
- update_conv_kernels: float32 [2304, 768], P(('fsdp', 'ctx'), 'tp')
- update_embed_table: float32 [51872, 768], P('tp', ('fsdp', 'ctx'))
- update_small_params: float32 [787, 768], replicated
- next_moment_projections: float32 [9, 768, 768], P(None, ('fsdp', 'ctx'), 'tp')
- next_moment_out_proj: float32 [3, 768, 768], P(None, ('fsdp', 'ctx'), 'tp')
- next_moment_feed_forward: float32 [4, 768, 3072], P(None, ('fsdp', 'ctx'), 'tp')
- next_moment_conv_kernels: float32 [2304, 768], P(('fsdp', 'ctx'), 'tp')
- next_moment_embed_table: float32 [51872, 768], P('tp', ('fsdp', 'ctx'))
- next_moment_small_params: float32 [787, 768], replicated
- next_average_projections: float32 [9, 768, 768], P(None, ('fsdp', 'ctx'), 'tp')
- next_average_out_proj: float32 [3, 768, 768], P(None, ('fsdp', 'ctx'), 'tp')
- next_average_feed_forward: float32 [4, 768, 3072], P(None, ('fsdp', 'ctx'), 'tp')
- next_average_conv_kernels: float32 [2304, 768], P(('fsdp', 'ctx'), 'tp')
- next_average_embed_table: float32 [51872, 768], P('tp', ('fsdp', 'ctx'))
- next_average_small_params: float32 [787, 768], replicated
The draws below stay inside these ranges and needn't reach their ends.
Inputs may be any that keep to these rules, and one draw needn't show every extreme that they name: `teach_rows`: for each clip and each c, the 64 entries of columns c * 64 to (c + 1) * 64 - 1 are distinct positions between c * 256 and (c + 1) * 256 - 1.
All inputs are finite; a program needn't handle non-finite values. No bound on the sum of `vocab_mask` on one device may be relied on, other than what follows from the above.
Results may differ from the reference program's by a relative error of at most 0.0085.
The reference program's roundings to bfloat16 on the way count: a program that leaves them out, or rounds other values in their place, can miss the bound.
Values may be sent and summed in bfloat16 or wider, within the bound.
A program may use at most 576 MiB of HBM per device.

```python
import math
import jax
import jax.numpy as jnp
from jax import lax

D = 768
H = 12
HD = 64
FF = 3072
V = 51872
MEL = 80
KW = 3
TOPK = 64
ENC = 1024
DEC = 512
CLIPS_ALL = 16
DEC_DEV = 256
KD = 128
KD_DEV = 64
NVEC = 35
NSMALL = 787


def small_rows(key):
    row_index = jnp.arange(NSMALL, dtype=jnp.int32)
    gain_rows = jnp.logical_and(row_index < 14, row_index % 2 == 0)
    kernel_rows = jnp.logical_and(row_index >= NVEC, row_index < NVEC + KW * MEL)
    position_rows = row_index >= NVEC + KW * MEL
    quiet_rows = jnp.logical_or(position_rows, row_index < 27)
    noise_draw = jnp.clip(jax.random.normal(key, (NSMALL, D), jnp.float32), -4.0, 4.0)
    spread = jnp.where(gain_rows, 0.2, jnp.where(kernel_rows, (KW * MEL) ** (-0.5), jnp.where(quiet_rows, 0.05, 0.3)))
    base_level = jnp.where(gain_rows, 1.0, 0.0)
    return base_level[:, None] + spread[:, None] * noise_draw


def draw_small_params(key, part):
    return small_rows(jax.random.fold_in(key, 17))


def draw_average_small_params(key, part):
    return small_rows(jax.random.fold_in(key, 29))


def draw_teach_rows(key, part):
    block_count = KD // KD_DEV
    total_blocks = CLIPS_ALL * block_count
    block_keys = jax.random.split(jax.random.fold_in(key, 5), total_blocks)
    block_place = jnp.arange(total_blocks, dtype=jnp.int32) % block_count
    slot_index = jnp.arange(DEC_DEV, dtype=jnp.int32)

    def one_block(block_key, place):
        ranking = jax.random.permutation(block_key, DEC_DEV).astype(jnp.int32)
        forced = jnp.where(place == 0, 0, jnp.where(place == block_count - 1, DEC_DEV - 1, -1)).astype(jnp.int32)
        ranking = jnp.where(slot_index == forced, -1, ranking)
        order = jnp.argsort(ranking, stable=True).astype(jnp.int32)
        return order[:KD_DEV]
    picked = jax.vmap(one_block)(block_keys, block_place).reshape(CLIPS_ALL, block_count, KD_DEV)
    offsets = jnp.arange(block_count, dtype=jnp.int32)[None, :, None] * DEC_DEV
    return (picked + offsets).reshape(CLIPS_ALL, KD).astype(jnp.int32)


def with_ends(values, stream_key, low, top_value):
    longest = values.shape.index(max(values.shape))
    spots = []
    for shift in (0, 1):
        where = [jax.random.randint(jax.random.fold_in(stream_key, axis), (), 0, length) for axis, length in enumerate(values.shape)]
        where[longest] = (where[longest] + shift) % values.shape[longest]
        spots.append(tuple(where))
    return values.at[spots[0]].set(low).at[spots[1]].set(top_value)


def block_levels(key, dims, shards, smallest, top_value):
    factor_of, own = 1.0, jax.random.fold_in(key, 6)
    for axis_at, shards_of in shards:
        steps = jnp.exp(jax.random.uniform(jax.random.fold_in(own, axis_at), (shards_of,), jnp.float32, smallest / len(shards), top_value / len(shards)))
        factor_of = factor_of * jnp.repeat(steps, dims[axis_at] // shards_of).reshape([-1 if axis == axis_at else 1 for axis in range(len(dims))])
    return factor_of


def bell_draw(own_key, extent, deviation, reach, pieces=(), kind=jnp.bfloat16):
    array = deviation * jax.random.normal(own_key, extent, jnp.float32)
    if pieces:
        array = array * block_levels(own_key, extent, pieces, -0.22, 0.18)
    return jnp.clip(array, -reach, reach).astype(kind)


def setup_inputs(seed: int = 0) -> dict:
    arg_keys = jax.random.split(jax.random.key(seed), 26)
    mel_frames = bell_draw(arg_keys[0], (CLIPS_ALL, 2 * ENC, MEL), 1.0, 6.0, ((0, 4), (1, 2)))
    dec_ids = with_ends(jax.random.randint(arg_keys[1], (CLIPS_ALL, DEC), 0, V), jax.random.fold_in(arg_keys[1], 1), 0, V - 1).astype(jnp.int32)
    targets = with_ends(jax.random.randint(arg_keys[2], (CLIPS_ALL, DEC), 0, V), jax.random.fold_in(arg_keys[2], 1), 0, V - 1).astype(jnp.int32)
    teach_rows = draw_teach_rows(jax.random.fold_in(arg_keys[25], 71), 0)
    teach_ids = with_ends(jax.random.randint(arg_keys[4], (CLIPS_ALL, KD, TOPK), 0, V), jax.random.fold_in(arg_keys[4], 1), 0, V - 1).astype(jnp.int32)
    teach_probs = jnp.clip(jnp.exp(math.log(0.03) - 2.70805 * jax.random.uniform(arg_keys[5], (CLIPS_ALL, KD, TOPK), jnp.float32) ** block_levels(arg_keys[5], (CLIPS_ALL, KD, TOPK), ((0, 4), (1, 2)), -0.2, 0.2)), 0.002, 0.03)
    vocab_mask = with_ends((jax.random.randint(arg_keys[6], (V,), 0, 8) < 7).astype(jnp.int32), jax.random.fold_in(arg_keys[6], 1), 0, 1)
    projections = bell_draw(arg_keys[7], (9, D, D), D ** -0.5, 0.21875, ((1, 8), (2, 4)), jnp.float32)
    out_proj = bell_draw(arg_keys[8], (3, D, D), (D // 16) ** -0.5, 0.875, ((1, 8), (2, 4)), jnp.float32)
    feed_forward = bell_draw(arg_keys[9], (4, D, FF), D ** -0.5, 0.21875, ((1, 8), (2, 4)), jnp.float32)
    conv_kernels = bell_draw(arg_keys[10], (KW * D, D), (KW * D) ** -0.5, 0.125, ((0, 8), (1, 4)), jnp.float32)
    embed_table = bell_draw(arg_keys[11], (V, D), (D // 8) ** -0.5, 0.625, ((0, 4), (1, 8)), jnp.float32)
    small_params = draw_small_params(jax.random.fold_in(arg_keys[25], 71), 0)
    moment_projections = bell_draw(arg_keys[13], (9, D, D), 0.0001, 0.00061035156, ((1, 8), (2, 4)), jnp.float32)
    moment_out_proj = bell_draw(arg_keys[14], (3, D, D), 0.0001, 0.00061035156, ((1, 8), (2, 4)), jnp.float32)
    moment_feed_forward = bell_draw(arg_keys[15], (4, D, FF), 0.0001, 0.00061035156, ((1, 8), (2, 4)), jnp.float32)
    moment_conv_kernels = bell_draw(arg_keys[16], (KW * D, D), 0.0001, 0.00061035156, ((0, 8), (1, 4)), jnp.float32)
    moment_embed_table = bell_draw(arg_keys[17], (V, D), 0.0001, 0.00061035156, ((0, 4), (1, 8)), jnp.float32)
    moment_small_params = bell_draw(arg_keys[18], (NSMALL, D), 0.0001, 0.00061035156, (), jnp.float32)
    average_projections = bell_draw(arg_keys[19], (9, D, D), D ** -0.5, 0.21875, ((1, 8), (2, 4)), jnp.float32)
    average_out_proj = bell_draw(arg_keys[20], (3, D, D), (D // 16) ** -0.5, 0.875, ((1, 8), (2, 4)), jnp.float32)
    average_feed_forward = bell_draw(arg_keys[21], (4, D, FF), D ** -0.5, 0.21875, ((1, 8), (2, 4)), jnp.float32)
    average_conv_kernels = bell_draw(arg_keys[22], (KW * D, D), (KW * D) ** -0.5, 0.125, ((0, 8), (1, 4)), jnp.float32)
    average_embed_table = bell_draw(arg_keys[23], (V, D), (D // 8) ** -0.5, 0.625, ((0, 4), (1, 8)), jnp.float32)
    average_small_params = draw_average_small_params(jax.random.fold_in(arg_keys[25], 71), 0)
    return dict(mel_frames=mel_frames, dec_ids=dec_ids, targets=targets, teach_rows=teach_rows, teach_ids=teach_ids, teach_probs=teach_probs, vocab_mask=vocab_mask, projections=projections, out_proj=out_proj, feed_forward=feed_forward, conv_kernels=conv_kernels, embed_table=embed_table, small_params=small_params, moment_projections=moment_projections, moment_out_proj=moment_out_proj, moment_feed_forward=moment_feed_forward, moment_conv_kernels=moment_conv_kernels, moment_embed_table=moment_embed_table, moment_small_params=moment_small_params, average_projections=average_projections, average_out_proj=average_out_proj, average_feed_forward=average_feed_forward, average_conv_kernels=average_conv_kernels, average_embed_table=average_embed_table, average_small_params=average_small_params)


@jax.custom_vjp
def low(v):
    return lax.optimization_barrier(v.astype(jnp.bfloat16)).astype(jnp.float32)

@jax.custom_vjp
def low_back(v):
    return v

def low_keep(v):
    return (low(v), None)

def low_pass(kept, grad):
    return (grad,)

def back_keep(v):
    return (v, None)

def back_low(kept, grad):
    return (low(grad),)
low.defvjp(low_keep, low_pass)
low_back.defvjp(back_keep, back_low)
EPSILON = 1e-05
CLIP_NORM = 1.0
MOMENTUM = 0.9
LEARN_RATE = 20.0
AVERAGE_RATE = 0.1
NEG_FILL = -1e+30

def matmul(left, right):
    return jnp.dot(left, right, precision=lax.Precision.HIGHEST)

def layer_norm(values, scale_row, shift_row):
    center = values - lax.optimization_barrier(jnp.mean(values, axis=-1, keepdims=True))
    spread = lax.optimization_barrier(jnp.mean(center * center, axis=-1, keepdims=True))
    return center * lax.rsqrt(spread + EPSILON) * scale_row + shift_row

def gelu_exact(values):
    return jax.nn.gelu(values, approximate=False)

def sinusoid(start, count, width):
    half_width = width // 2
    increment = math.log(10000.0) / (half_width - 1)
    inverse = jnp.exp(-increment * jnp.arange(half_width, dtype=jnp.int32).astype(jnp.float32))
    moments = (start + jnp.arange(count, dtype=jnp.int32)).astype(jnp.float32)
    angles = moments[:, None] * inverse[None, :]
    return jnp.concatenate([jnp.sin(angles), jnp.cos(angles)], axis=1)

def attention(query_in, key_in, weight_set, bias_set, out_weight, out_bias, causal):
    query_count = query_in.shape[0]
    key_count = key_in.shape[0]
    queries = low(low_back(matmul(query_in, weight_set[0]) + bias_set[0])).reshape(query_count, H, HD)
    keys_all = low(low_back(matmul(key_in, weight_set[1]))).reshape(key_count, H, HD)
    values_all = low(low_back(matmul(key_in, weight_set[2]) + bias_set[1])).reshape(key_count, H, HD)
    scores = jnp.einsum('qhd,khd->hqk', queries, keys_all, precision=lax.Precision.HIGHEST)
    scores = low_back(scores * HD ** (-0.5))
    if causal:
        allowed = jnp.arange(key_count, dtype=jnp.int32)[None, :] <= jnp.arange(query_count, dtype=jnp.int32)[:, None]
        scores = jnp.where(allowed[None], scores, NEG_FILL)
    weights_low = low(jax.nn.softmax(scores, axis=-1))
    mixed = jnp.einsum('hqk,khd->qhd', weights_low, values_all, precision=lax.Precision.HIGHEST)
    mixed = low(low_back(mixed.reshape(query_count, H * HD)))
    return low_back(matmul(mixed, out_weight.T) + out_bias)

def feed_block(inputs, weight_in, bias_in, weight_out, bias_out):
    hidden = low_back(matmul(inputs, weight_in) + bias_in)
    active = low(gelu_exact(hidden))
    return low_back(matmul(active, weight_out.T) + bias_out)

def clip_terms(params, mel_clip, ids_clip, target_clip, rows_clip, teach_id_clip, teach_prob_clip, mask_open):
    projections, out_proj, feed_forward, conv_kernels, embed_table, small_f, kernel_one = params
    frames = mel_clip.astype(jnp.float32)
    padded = jnp.pad(frames, ((1, 1), (0, 0)))
    taps_one = jnp.concatenate([padded[tap_index:tap_index + 2 * ENC] for tap_index in range(KW)], axis=1)
    first_conv = low_back(matmul(taps_one, kernel_one) + small_f[14])
    first_conv = low(gelu_exact(first_conv))
    padded_two = jnp.pad(first_conv, ((1, 1), (0, 0)))
    taps_two = jnp.concatenate([padded_two[tap_index:tap_index + 2 * ENC:2] for tap_index in range(KW)], axis=1)
    second_kernel = conv_kernels.reshape(KW, D, D).transpose(0, 2, 1).reshape(KW * D, D)
    second_conv = low_back(matmul(taps_two, second_kernel) + small_f[15])
    stream = gelu_exact(second_conv) + sinusoid(0, ENC, D)
    hidden_bias = small_f[27:NVEC].reshape(2, FF)
    attn_in = low(layer_norm(stream, small_f[0], small_f[1]))
    stream = stream + attention(attn_in, attn_in, (projections[0], projections[1], projections[2]), (small_f[16], small_f[17]), out_proj[0], small_f[18], False)
    feed_in = low(layer_norm(stream, small_f[2], small_f[3]))
    stream = stream + feed_block(feed_in, feed_forward[0], hidden_bias[0], feed_forward[1], small_f[19])
    encoded = low(layer_norm(stream, small_f[4], small_f[5]))
    tokens = low_back(embed_table[ids_clip]) + small_f[NVEC + KW * MEL:]
    norm_one = low(layer_norm(tokens, small_f[6], small_f[7]))
    tokens = tokens + attention(norm_one, norm_one, (projections[3], projections[4], projections[5]), (small_f[20], small_f[21]), out_proj[1], small_f[22], True)
    norm_two = low(layer_norm(tokens, small_f[8], small_f[9]))
    tokens = tokens + attention(norm_two, encoded, (projections[6], projections[7], projections[8]), (small_f[23], small_f[24]), out_proj[2], small_f[25], False)
    norm_three = low(layer_norm(tokens, small_f[10], small_f[11]))
    tokens = tokens + feed_block(norm_three, feed_forward[2], hidden_bias[1], feed_forward[3], small_f[26])
    final_norm = low(layer_norm(tokens, small_f[12], small_f[13]))
    logits = low_back(matmul(final_norm, embed_table.T))
    masked = jnp.where(mask_open[None, :], logits, NEG_FILL)
    log_total = jax.nn.logsumexp(masked, axis=-1)
    picked = jnp.take_along_axis(logits, target_clip[:, None], axis=1)[:, 0]
    cross_sum = jnp.sum(log_total - picked)
    teach_logits = logits[rows_clip[:, None], teach_id_clip]
    teach_lse = log_total[rows_clip]
    teach_sum = jnp.sum(teach_prob_clip * (jnp.log(teach_prob_clip) - (teach_logits - teach_lse[:, None])))
    return (cross_sum, teach_sum)

def nesterov(weight, grad, moment, average, factor):
    clipped = grad * factor
    moment_new = MOMENTUM * moment + clipped
    change = -LEARN_RATE * (clipped + MOMENTUM * moment_new)
    average_new = average + AVERAGE_RATE * (weight + change - average)
    return (change, moment_new, average_new)

def reference(mel_frames, dec_ids, targets, teach_rows, teach_ids, teach_probs, vocab_mask, projections, out_proj, feed_forward, conv_kernels, embed_table, small_params, moment_projections, moment_out_proj, moment_feed_forward, moment_conv_kernels, moment_embed_table, moment_small_params, average_projections, average_out_proj, average_feed_forward, average_conv_kernels, average_embed_table, average_small_params):
    mask_open = vocab_mask > 0
    clip_total = mel_frames.shape[0]

    def forward(proj_f, out_f, feed_f, conv_f, table_f, small_f):
        params = (low(proj_f), low(out_f), low(feed_f), low(conv_f), low(table_f), small_f, low(small_f[NVEC:NVEC + KW * MEL]))

        def one_clip(inputs):
            return clip_terms(params, inputs[0], inputs[1], inputs[2], inputs[3], inputs[4], inputs[5], mask_open)
        cross_sums, teach_sums = lax.map(jax.checkpoint(one_clip), (mel_frames, dec_ids, targets, teach_rows, teach_ids, teach_probs))
        return jnp.sum(cross_sums) / (clip_total * DEC) + jnp.sum(teach_sums) / (clip_total * KD)
    loss, pullback = jax.vjp(forward, projections, out_proj, feed_forward, conv_kernels, embed_table, small_params)
    grads = pullback(jnp.ones((), jnp.float32))
    squares = jnp.zeros((), jnp.float32)
    for grad_item in grads:
        squares = squares + jnp.sum(grad_item * grad_item)
    grad_norm = jnp.sqrt(squares)
    factor = jnp.minimum(1.0, CLIP_NORM / (grad_norm + 1e-06))
    next_proj = nesterov(projections, grads[0], moment_projections, average_projections, factor)
    next_out = nesterov(out_proj, grads[1], moment_out_proj, average_out_proj, factor)
    next_feed = nesterov(feed_forward, grads[2], moment_feed_forward, average_feed_forward, factor)
    next_conv = nesterov(conv_kernels, grads[3], moment_conv_kernels, average_conv_kernels, factor)
    next_table = nesterov(embed_table, grads[4], moment_embed_table, average_embed_table, factor)
    next_small = nesterov(small_params, grads[5], moment_small_params, average_small_params, factor)
    return (loss, grad_norm, next_proj[0], next_out[0], next_feed[0], next_conv[0], next_table[0], next_small[0], next_proj[1], next_out[1], next_feed[1], next_conv[1], next_table[1], next_small[1], next_proj[2], next_out[2], next_feed[2], next_conv[2], next_table[2], next_small[2])
```

```python
import functools
import math

import jax
import jax.numpy as jnp
from jax import lax
from jax.experimental import pallas as pl
from jax.experimental.pallas import tpu as pltpu
from jax.sharding import PartitionSpec as P

D = 768
H = 12
HD = 64
FF = 3072
MEL = 80
KW = 3
NVEC = 35
EPSILON = 1e-05
CLIP_NORM = 1.0
MOMENTUM = 0.9
LEARN_RATE = 20.0
AVERAGE_RATE = 0.1
NEG_FILL = -1e30
CHUNK = 512
LANES = 128
VMEM_LIMIT = 56 * 1024 * 1024
PLANE = ("ctx", "tp")
ALL = ("fsdp", "ctx", "tp")


def to_low(values):
    return values.astype(jnp.bfloat16)


def product(pattern, left, right):
    return jnp.einsum(pattern, left, right, preferred_element_type=jnp.float32)


def layer_norm(values, scale_row, shift_row):
    center = values - jnp.mean(values, axis=-1, keepdims=True)
    spread = jnp.mean(center * center, axis=-1, keepdims=True)
    return center * lax.rsqrt(spread + EPSILON) * scale_row + shift_row


def norm_back(values, scale_row, shift_row, upstream):
    unused_out, pullback = jax.vjp(layer_norm, values, scale_row, shift_row)
    return pullback(upstream)


def gelu_exact(values):
    return jax.nn.gelu(values, approximate=False)


def gelu_back(values, upstream):
    unused_out, pullback = jax.vjp(gelu_exact, values)
    return pullback(upstream)[0]


def sinusoid(start, count, width):
    half_width = width // 2
    increment = math.log(10000.0) / (half_width - 1)
    inverse = jnp.exp(-increment * jnp.arange(half_width, dtype=jnp.int32).astype(jnp.float32))
    moments = (start + jnp.arange(count, dtype=jnp.int32)).astype(jnp.float32)
    angles = moments[:, None] * inverse[None, :]
    return jnp.concatenate([jnp.sin(angles), jnp.cos(angles)], axis=1)


def pick(values, index):
    return lax.dynamic_index_in_dim(values, index, 0, keepdims=False)


def place(values, part, index):
    return lax.dynamic_update_index_in_dim(values, part, index, 0)


def shifted(axis, step):
    count = lax.axis_size(axis)
    return [(i, (i + step) % count) for i in range(count)]


def in_order(arrived, axis):
    count = len(arrived)
    index = lax.axis_index(axis)
    if count == 2:
        return jnp.where(index == 0, jnp.stack(arrived), jnp.stack(arrived[::-1]))
    out = jnp.zeros((count,) + arrived[0].shape, arrived[0].dtype)
    for step, piece in enumerate(arrived):
        out = place(out, piece, lax.rem(index - step + count, count))
    return out


def sent_to_all(values, axis):
    count = lax.axis_size(axis)
    return [values] + [
        lax.ppermute(values, axis, shifted(axis, step)) for step in range(1, count)
    ]


def spread(values, axis):
    return in_order(sent_to_all(values, axis), axis)


def sent_to_owners(pieces_for, axis):
    count = lax.axis_size(axis)
    return [pieces_for(0)] + [
        lax.ppermute(pieces_for(step), axis, shifted(axis, step)) for step in range(1, count)
    ]


def wide_sum(pieces):
    total = pieces[0].astype(jnp.float32)
    for piece in pieces[1:]:
        total = total + piece.astype(jnp.float32)
    return total


def sum_to_owner(values, axis):
    count = lax.axis_size(axis)
    index = lax.axis_index(axis)
    return wide_sum(
        sent_to_owners(lambda step: pick(values, lax.rem(index + step, count)), axis)
    )


def together(*values):
    return lax.optimization_barrier(values)


def exchanged_sum(values, axes):
    for axis in axes:
        count = lax.axis_size(axis)
        bit = 1
        while bit < count:
            values = values + lax.ppermute(values, axis, [(i, i ^ bit) for i in range(count)])
            bit *= 2
    return values


def head_scores(queries, keys, key_place, query_place):
    scores = product("qhd,khd->hqk", queries, keys) * HD ** (-0.5)
    if key_place is not None:
        allowed = key_place[None, :] <= query_place[:, None]
        scores = jnp.where(allowed[None], scores, NEG_FILL)
    return scores


def split_heads(values):
    return values.reshape(values.shape[0], H, HD)


def attention_forward(rows_q, rows_k, weights, biases, key_place, query_place):
    queries = split_heads(to_low(product("qd,dh->qh", rows_q, weights[0]) + biases[0]))
    keys = split_heads(to_low(product("qd,dh->qh", rows_k, weights[1])))
    values = split_heads(to_low(product("qd,dh->qh", rows_k, weights[2]) + biases[1]))
    scores = head_scores(queries, keys, key_place, query_place)
    top = jnp.max(scores, axis=-1, keepdims=True)
    raised = jnp.exp(scores - top)
    total = jnp.sum(raised, axis=-1, keepdims=True)
    mixed = product("hqk,khd->qhd", to_low(raised / total), values)
    mixed = to_low(mixed.reshape(rows_q.shape))
    out = product("qh,oh->qo", mixed, weights[3]) + biases[2]
    return out, (queries, keys, values, mixed, top + jnp.log(total))


def attention_backward(rows_q, rows_k, weights, saved, grad_out, key_place, query_place):
    queries, keys, values, mixed, log_total = saved
    grad_out_weight = product("qo,qh->oh", grad_out, mixed)
    grad_mixed = split_heads(to_low(product("qo,oh->qh", grad_out, weights[3])))
    scores = head_scores(queries, keys, key_place, query_place)
    probs = jnp.exp(scores - log_total)
    grad_probs = product("qhd,khd->hqk", grad_mixed, values)
    inner = jnp.sum(probs * grad_probs, axis=-1, keepdims=True)
    grad_scores = to_low(probs * (grad_probs - inner))
    factor = HD ** (-0.5)
    grad_q = to_low(product("hqk,khd->qhd", grad_scores, keys) * factor).reshape(rows_q.shape)
    grad_k = to_low(product("hqk,qhd->khd", grad_scores, queries) * factor).reshape(rows_k.shape)
    grad_v = to_low(product("hqk,qhd->khd", to_low(probs), grad_mixed)).reshape(rows_k.shape)
    grad_weights = (
        product("qd,qh->dh", rows_q, grad_q),
        product("qd,qh->dh", rows_k, grad_k),
        product("qd,qh->dh", rows_k, grad_v),
        grad_out_weight,
    )
    bias_q = jnp.sum(grad_q, axis=0, dtype=jnp.float32)
    bias_v = jnp.sum(grad_v, axis=0, dtype=jnp.float32)
    back_q = product("qh,dh->qd", grad_q, weights[0])
    back_k = product("qh,dh->qd", grad_k, weights[1]) + product("qh,dh->qd", grad_v, weights[2])
    return grad_weights, bias_q, bias_v, back_q, back_k


def feed_forward_pass(rows, weight_in, bias_in, weight_out, bias_out):
    hidden = product("qd,df->qf", rows, weight_in) + bias_in
    active = to_low(gelu_exact(hidden))
    return product("qf,of->qo", active, weight_out) + bias_out, (hidden, active)


def feed_backward(rows, weight_in, weight_out, saved, grad_out):
    hidden, active = saved
    grad_weight_out = product("qo,qf->of", grad_out, active)
    grad_active = product("qo,of->qf", grad_out, weight_out)
    grad_hidden = to_low(gelu_back(hidden, grad_active))
    grad_weight_in = product("qd,qf->df", rows, grad_hidden)
    grad_bias_in = jnp.sum(grad_hidden, axis=0, dtype=jnp.float32)
    back = product("qf,df->qd", grad_hidden, weight_in)
    return grad_weight_in, grad_weight_out, grad_bias_in, back


def nesterov(weight, grad, moment, average, factor):
    clipped = grad * factor
    moment_new = MOMENTUM * moment + clipped
    change = -LEARN_RATE * (clipped + MOMENTUM * moment_new)
    average_new = average + AVERAGE_RATE * (weight + change - average)
    return (change, moment_new, average_new)


def stats_kernel(
    blocks, rows, teach, final_ref, bias_ref, target_ref, weight_ref, table_ref,
    top_ref, total_ref, pick_ref, dot_ref,
):
    chunk = table_ref.shape[1]
    tiles = chunk // LANES

    @pl.when(pl.program_id(0) == 0)
    def _():
        top_ref[...] = jnp.full(top_ref.shape, 2.0 * NEG_FILL, jnp.float32)
        total_ref[...] = jnp.zeros(total_ref.shape, jnp.float32)
        pick_ref[...] = jnp.zeros(pick_ref.shape, jnp.float32)
        dot_ref[...] = jnp.zeros(dot_ref.shape, jnp.float32)

    start = pl.program_id(0) * chunk
    for block in range(blocks):
        span = pl.ds(block * rows, rows)
        logits = jnp.dot(final_ref[span, :], table_ref[...], preferred_element_type=jnp.float32)
        target = target_ref[span, :] - start
        top_old = top_ref[span, :]
        masked = []
        picked = pick_ref[span, :]
        top_new = top_old
        dots = dot_ref[...]
        for tile in range(tiles):
            lanes = slice(tile * LANES, (tile + 1) * LANES)
            piece = logits[:, lanes]
            column = lax.broadcasted_iota(jnp.int32, (rows, LANES), 1) + tile * LANES
            picked = picked + jnp.where(column == target, piece, 0.0)
            dots = dots + piece[:teach] * weight_ref[
                tile, pl.ds(block * teach, teach), :
            ].astype(jnp.float32)
            piece = piece + bias_ref[:, lanes]
            masked.append(piece)
            top_new = jnp.maximum(top_new, piece)
        total = total_ref[span, :] * jnp.exp(top_old - top_new)
        for piece in masked:
            total = total + jnp.exp(piece - top_new)
        top_ref[span, :] = top_new
        total_ref[span, :] = total
        pick_ref[span, :] = picked
        dot_ref[...] = dots


def loss_stats(final_all, table, bias_row, targets, weights, blocks):
    count = final_all.shape[0]
    width = table.shape[1]
    rows = count // blocks
    teach = weights.shape[1] // blocks
    whole = lambda j: (0, 0)
    by_chunk = lambda j: (0, j)
    row_stat = jax.ShapeDtypeStruct((count, LANES), jnp.float32)
    return pl.pallas_call(
        functools.partial(stats_kernel, blocks, rows, teach),
        grid=(width // CHUNK,),
        in_specs=[
            pl.BlockSpec((count, D), whole),
            pl.BlockSpec((1, CHUNK), by_chunk),
            pl.BlockSpec((count, 1), whole),
            pl.BlockSpec((CHUNK // LANES, weights.shape[1], LANES), lambda j: (j, 0, 0)),
            pl.BlockSpec((D, CHUNK), by_chunk),
        ],
        out_specs=[
            pl.BlockSpec((count, LANES), whole),
            pl.BlockSpec((count, LANES), whole),
            pl.BlockSpec((count, LANES), whole),
            pl.BlockSpec((teach, LANES), whole),
        ],
        out_shape=[
            row_stat,
            row_stat,
            row_stat,
            jax.ShapeDtypeStruct((teach, LANES), jnp.float32),
        ],
        compiler_params=pltpu.CompilerParams(
            vmem_limit_bytes=VMEM_LIMIT, dimension_semantics=("arbitrary",)
        ),
        cost_estimate=pl.CostEstimate(
            flops=2 * count * D * width,
            bytes_accessed=2 * (D + weights.shape[1]) * width,
            transcendentals=count * width,
        ),
        name="loss_stats",
    )(final_all, bias_row, targets, weights, table)


def grads_kernel(
    blocks, rows, teach, token_share, final_ref, flipped_ref, bias_ref, target_ref, level_ref,
    weight_ref, table_ref, final_grad_ref, table_grad_ref, low_ref,
):
    chunk = table_ref.shape[1]
    start = pl.program_id(0) * chunk

    @pl.when(pl.program_id(0) == 0)
    def _():
        final_grad_ref[...] = jnp.zeros(final_grad_ref.shape, jnp.float32)

    for block in range(blocks):
        span = pl.ds(block * rows, rows)
        logits = jnp.dot(final_ref[span, :], table_ref[...], preferred_element_type=jnp.float32)
        column = lax.broadcasted_iota(jnp.int32, (rows, chunk), 1)
        target = target_ref[span, :] - start
        grad = jnp.exp(logits + bias_ref[...] - level_ref[span, :])
        grad = grad - jnp.where(column == target, token_share, 0.0)
        for tile in range(chunk // LANES):
            lanes = slice(tile * LANES, (tile + 1) * LANES)
            weight = weight_ref[tile, pl.ds(block * teach, teach), :].astype(jnp.float32)
            low_ref[pl.ds(block * rows, teach), lanes] = to_low(grad[:teach, lanes] - weight)
        low_ref[pl.ds(block * rows + teach, rows - teach), :] = to_low(grad[teach:])
        final_grad_ref[span, :] += lax.dot_general(
            low_ref[span, :],
            table_ref[...],
            (((1,), (1,)), ((), ())),
            preferred_element_type=jnp.float32,
        )
    table_grad_ref[...] = to_low(
        jnp.dot(flipped_ref[...], low_ref[...], preferred_element_type=jnp.float32)
    )


def loss_grads(final_all, table, bias_row, targets, levels, weights, blocks, token_share):
    count = final_all.shape[0]
    width = table.shape[1]
    rows = count // blocks
    teach = weights.shape[1] // blocks
    whole = lambda j: (0, 0)
    by_chunk = lambda j: (0, j)
    return pl.pallas_call(
        functools.partial(grads_kernel, blocks, rows, teach, token_share),
        grid=(width // CHUNK,),
        in_specs=[
            pl.BlockSpec((count, D), whole),
            pl.BlockSpec((D, count), whole),
            pl.BlockSpec((1, CHUNK), by_chunk),
            pl.BlockSpec((count, 1), whole),
            pl.BlockSpec((count, 1), whole),
            pl.BlockSpec((CHUNK // LANES, weights.shape[1], LANES), lambda j: (j, 0, 0)),
            pl.BlockSpec((D, CHUNK), by_chunk),
        ],
        out_specs=[pl.BlockSpec((count, D), whole), pl.BlockSpec((D, CHUNK), by_chunk)],
        out_shape=[
            jax.ShapeDtypeStruct((count, D), jnp.float32),
            jax.ShapeDtypeStruct((D, width), jnp.bfloat16),
        ],
        scratch_shapes=[pltpu.VMEM((count, CHUNK), jnp.bfloat16)],
        compiler_params=pltpu.CompilerParams(
            vmem_limit_bytes=VMEM_LIMIT, dimension_semantics=("arbitrary",)
        ),
        cost_estimate=pl.CostEstimate(
            flops=6 * count * D * width,
            bytes_accessed=2 * (2 * D + weights.shape[1]) * width + 4 * count * D,
            transcendentals=count * width,
        ),
        name="loss_grads",
    )(final_all, final_all.T, bias_row, targets, levels, weights, table)


def lookup_kernel(place_ref, table_ref, out_ref):
    def some(group, carry):
        for at in range(16):
            row = group * 16 + at
            out_ref[pl.ds(row, 1), :] = table_ref[pl.ds(place_ref[row], 1), :]
        return carry

    lax.fori_loop(0, out_ref.shape[0] // 16, some, 0)


def lookup(places, table):
    count, width = places.shape[0], table.shape[1]
    return pl.pallas_call(
        lookup_kernel,
        out_shape=jax.ShapeDtypeStruct((count, width), jnp.float32),
        in_specs=[
            pl.BlockSpec(memory_space=pltpu.SMEM),
            pl.BlockSpec(memory_space=pltpu.VMEM),
        ],
        out_specs=pl.BlockSpec(memory_space=pltpu.VMEM),
        compiler_params=pltpu.CompilerParams(vmem_limit_bytes=VMEM_LIMIT),
        cost_estimate=pl.CostEstimate(
            flops=count * width, bytes_accessed=70_000_000, transcendentals=0
        ),
        name="lookup",
    )(places, table)


def scatter_kernel(place_ref, grad_ref, out_ref, *sum_refs):
    streams = len(sum_refs)
    for sum_ref in sum_refs:
        sum_ref[...] = jnp.zeros(sum_ref.shape, jnp.float32)
    run = grad_ref.shape[0] // streams

    def some(group, carry):
        for at in range(4):
            for stream, sum_ref in enumerate(sum_refs):
                row = stream * run + group * 4 + at
                sum_ref[pl.ds(place_ref[row], 1), :] += grad_ref[pl.ds(row, 1), :]
        return carry

    lax.fori_loop(0, run // 4, some, 0)
    total = sum_refs[0][: out_ref.shape[0], :]
    for sum_ref in sum_refs[1:]:
        total = total + sum_ref[: out_ref.shape[0], :]
    out_ref[...] = total


def scatter_add(places, grads, height):
    count, width = grads.shape
    return pl.pallas_call(
        scatter_kernel,
        out_shape=jax.ShapeDtypeStruct((height, width), jnp.float32),
        in_specs=[
            pl.BlockSpec(memory_space=pltpu.SMEM),
            pl.BlockSpec(memory_space=pltpu.VMEM),
        ],
        out_specs=pl.BlockSpec(memory_space=pltpu.VMEM),
        scratch_shapes=[pltpu.VMEM((height + 8, width), jnp.float32)] * 4,
        compiler_params=pltpu.CompilerParams(vmem_limit_bytes=VMEM_LIMIT),
        cost_estimate=pl.CostEstimate(
            flops=count * width, bytes_accessed=90_000_000, transcendentals=0
        ),
        name="scatter_add",
    )(places, grads)


def local(
    mel_frames,
    dec_ids,
    targets,
    teach_rows,
    teach_ids,
    teach_probs,
    vocab_mask,
    projections,
    out_proj,
    feed_forward,
    conv_kernels,
    embed_table,
    small_params,
    moment_projections,
    moment_out_proj,
    moment_feed_forward,
    moment_conv_kernels,
    moment_embed_table,
    moment_small_params,
    average_projections,
    average_out_proj,
    average_feed_forward,
    average_conv_kernels,
    average_embed_table,
    average_small_params,
):
    fsdp_count, ctx_count, tp_count = (lax.axis_size(axis) for axis in ALL)
    fsdp_index, ctx_index, tp_index = (lax.axis_index(axis) for axis in ALL)
    clip_count = mel_frames.shape[0]
    blocks = ctx_count * tp_count
    part_count = ctx_count
    paired = ctx_count == 2 and tp_count % 2 == 0
    block_index = ctx_index * tp_count + tp_index
    if paired:
        clip_index, part_index = block_index // 2, block_index % 2
        part_of_block = jnp.arange(blocks, dtype=jnp.int32) % 2
    else:
        clip_index, part_index = tp_index, ctx_index
        part_of_block = jnp.arange(blocks, dtype=jnp.int32) // tp_count

    def in_blocks(values):
        if paired:
            values = jnp.swapaxes(values, 0, 1)
        return values.reshape((blocks,) + values.shape[2:])

    pairs = [(i, i ^ 1) for i in range(tp_count)]

    def spread_rows(rows):
        if paired:
            return jnp.concatenate([rows, lax.ppermute(rows, "tp", pairs)], axis=0)
        return lax.all_gather(rows, "ctx", axis=0, tiled=True)

    def collect_rows(rows):
        if paired:
            half = rows.shape[0] // 2
            other = lax.ppermute(to_low(rows[half:]), "tp", pairs)
            return rows[:half] + other.astype(jnp.float32)
        return lax.psum_scatter(to_low(rows), "ctx", scatter_dimension=0, tiled=True).astype(
            jnp.float32
        )

    enc_rows = mel_frames.shape[1] // 2
    dec_rows = dec_ids.shape[1]
    teach_count = teach_rows.shape[1]
    vocab_local = embed_table.shape[0]

    piece = D // (fsdp_count * ctx_count * tp_count)
    thick = D // (fsdp_count * ctx_count)

    def by_owner(values):
        count, height, width = values.shape
        return values.reshape(count, tp_count, height // tp_count, width).swapaxes(0, 1)

    def swapped_rows(values):
        arrived = lax.all_to_all(values, "tp", 0, 0, tiled=True)
        return arrived.transpose(1, 2, 0, 3).reshape(arrived.shape[1], arrived.shape[2], D)

    narrow_attn = by_owner(jnp.concatenate([to_low(projections), to_low(out_proj)], axis=0))
    narrow_conv = by_owner(to_low(conv_kernels)[None])
    narrow_conv = narrow_conv.reshape(tp_count, KW, piece, D // tp_count)
    own_rows = swapped_rows(jnp.concatenate([narrow_attn, narrow_conv], axis=1))
    feed_low = to_low(feed_forward)

    groups = (
        ((0, 1, 2, 9), (), True),
        ((), (0, 1), False),
        ((3, 4, 5, 10, 6, 7, 8, 11), (), False),
        ((), (2, 3), False),
    )
    narrow_full, feed_full = {}, {}
    stacks = []
    for narrow_members, feed_members, with_conv in groups:
        parts = []
        if with_conv:
            parts.append(own_rows[12:].reshape(KW * piece, D))
        parts += [own_rows[member] for member in narrow_members]
        parts += [feed_low[member] for member in feed_members]
        stacks.append(jnp.concatenate(parts, axis=0))
    held_of = [spread(stack, "fsdp") for stack in stacks]

    def plane_full(held):
        return lax.all_gather(held, PLANE, axis=0).reshape(
            (ctx_count, tp_count) + held.shape
        )

    def unpack(group, full):
        narrow_members, feed_members, with_conv = group
        offset = KW * piece if with_conv else 0
        for member in narrow_members:
            narrow_full[member] = (
                full[:, :, :, offset : offset + piece].transpose(2, 0, 1, 3, 4).reshape(D, D)
            )
            offset += piece
        for member in feed_members:
            feed_full[member] = (
                full[:, :, :, offset : offset + thick].transpose(2, 0, 3, 1, 4).reshape(D, FF)
            )
            offset += thick

    vocab_part = -(-vocab_local // (ctx_count * CHUNK)) * CHUNK
    table_low = to_low(embed_table)
    table_wide = jnp.pad(table_low.T, ((0, 0), (0, ctx_count * vocab_part - vocab_local)))

    def vocab_slice(step):
        start = lax.rem(ctx_index + step, ctx_count) * vocab_part
        return lax.dynamic_slice_in_dim(table_wide, start, vocab_part, 1)

    table_held = in_order(sent_to_owners(vocab_slice, "ctx"), "ctx")
    table_held = table_held.reshape(ctx_count * thick, vocab_part)

    held_of[0], dec_ids = together(held_of[0], dec_ids)
    full = plane_full(held_of[0])
    conv_full = full[:, :, :, : KW * piece].transpose(2, 0, 1, 3, 4).reshape(KW, D, D)
    unpack(groups[0], full)
    ids_plane = spread(jnp.stack([dec_ids, targets]), "ctx")
    ids_all = spread(in_blocks(ids_plane[:, 0]), "fsdp").reshape(
        fsdp_count, ctx_count, tp_count, dec_rows
    )
    target_blocks = in_blocks(ids_plane[:, 1])

    ids_local = ids_all.transpose(2, 0, 1, 3).reshape(-1) - tp_index * vocab_local
    ids_inside = jnp.logical_and(ids_local >= 0, ids_local < vocab_local)
    looked = lookup(jnp.where(ids_inside, ids_local, 0), embed_table)
    looked = to_low(jnp.where(ids_inside[:, None], looked, 0.0))
    looked = looked.reshape(tp_count, fsdp_count * ctx_count * dec_rows, thick)
    looked = lax.psum_scatter(looked, "tp", scatter_dimension=0, tiled=False)
    looked = looked.reshape(fsdp_count * ctx_count, dec_rows, thick)
    looked = lax.all_to_all(looked, ("fsdp", "ctx"), 0, 0, tiled=True)
    embedded = looked.transpose(1, 0, 2).reshape(dec_rows, D).astype(jnp.float32)

    packed = jnp.concatenate(
        [
            teach_probs,
            teach_ids.astype(jnp.float32),
            teach_rows[..., None].astype(jnp.float32),
        ],
        axis=2,
    )
    packed, held_of[2] = together(packed, held_of[2])
    unpack(groups[2], plane_full(held_of[2]))
    packed = in_blocks(spread(packed, "ctx"))
    top_count = teach_probs.shape[2]
    taught = (
        packed[:, :, -1].astype(jnp.int32),
        packed[:, :, top_count : 2 * top_count].astype(jnp.int32),
        packed[:, :, :top_count],
    )
    token_total = clip_count * fsdp_count * dec_rows * ctx_count
    teach_total = clip_count * fsdp_count * teach_count * ctx_count
    token_share = 1.0 / token_total
    row_place = jnp.arange(dec_rows, dtype=jnp.int32)
    taught_rows = taught[0] - part_of_block[:, None] * dec_rows
    hits = taught_rows[:, :, None] == row_place[None, None, :]
    rank_taught = jnp.sum(
        jnp.where(hits, jnp.arange(teach_count, dtype=jnp.int32)[None, :, None], 0), axis=1
    )
    is_taught = jnp.any(hits, axis=1)
    earlier = row_place[None, :, None] < row_place[None, None, :]
    rank_other = teach_count + jnp.sum(
        jnp.where(jnp.logical_and(earlier, ~is_taught[:, :, None]), 1, 0), axis=1
    )
    new_place = jnp.where(is_taught, rank_taught, rank_other)
    moved = new_place[:, None, :] == row_place[None, :, None]
    vocab_start = tp_index * vocab_local + ctx_index * vocab_part
    vocab_valid = jnp.minimum(vocab_part, vocab_local - ctx_index * vocab_part)
    target_local = (
        jnp.sum(jnp.where(moved, target_blocks[:, None, :], 0), axis=2) - vocab_start
    )
    target_local = jnp.where(
        jnp.logical_and(target_local >= 0, target_local < vocab_valid), target_local, -1
    ).reshape(-1, 1)
    share_taught = taught[2] / teach_total
    row_weight = jnp.concatenate(
        [
            token_share + jnp.sum(share_taught, axis=2),
            jnp.full((blocks, dec_rows - teach_count), token_share, jnp.float32),
        ],
        axis=1,
    ).reshape(-1)
    taught_local = (taught[1] - vocab_start).reshape(blocks * teach_count, -1)
    inside = jnp.logical_and(taught_local >= 0, taught_local < vocab_valid)
    high = jnp.where(inside, taught_local // LANES, -1)
    low_part = taught_local - taught_local // LANES * LANES
    high_hot = jnp.where(
        high[:, None, :] == jnp.arange(vocab_part // LANES, dtype=jnp.int32)[None, :, None],
        share_taught.reshape(blocks * teach_count, 1, -1),
        0.0,
    ).astype(jnp.bfloat16)
    low_hot = (
        low_part[:, None, :] == jnp.arange(LANES, dtype=jnp.int32)[None, :, None]
    ).astype(jnp.bfloat16)
    teach_weight = to_low(product("rhk,rlk->hrl", high_hot, low_hot))
    mask_wide = jnp.pad(vocab_mask, (0, ctx_count * vocab_part - vocab_local))
    mask_part = lax.dynamic_slice_in_dim(mask_wide, ctx_index * vocab_part, vocab_part, 0)
    bias_row = jnp.where(mask_part > 0, 0.0, NEG_FILL).astype(jnp.float32)[None, :]

    if paired:
        partner_block = (1 - ctx_index) * tp_count + tp_index
        mine = pick(mel_frames, clip_index)
        arrived = lax.ppermute(pick(mel_frames, partner_block // 2), "ctx", [(0, 1), (1, 0)])
        clip_mel = jnp.where(
            ctx_index == 0,
            jnp.concatenate([mine, arrived], axis=0),
            jnp.concatenate([arrived, mine], axis=0),
        )
    else:
        clip_mel = lax.all_gather(pick(mel_frames, clip_index), "ctx", axis=0, tiled=True)
    frame_pairs = jnp.pad(clip_mel.reshape(-1, 2 * MEL), ((1, 1), (0, 0)))
    near = lax.dynamic_slice_in_dim(frame_pairs, part_index * enc_rows, enc_rows + 2, 0)
    evens, odds = near[:, :MEL], near[:, MEL:]
    evens, odds, held_of[1] = together(evens, odds, held_of[1])
    unpack(groups[1], plane_full(held_of[1]))
    taps_even = jnp.concatenate([odds[:-2], evens[1:-1], odds[1:-1]], axis=1)
    taps_odd = jnp.concatenate([evens[:-1], odds[:-1], evens[1:]], axis=1)

    hidden_bias = small_params[27:NVEC].reshape(2, FF)
    kernel_one = to_low(small_params[NVEC : NVEC + KW * MEL])
    pre_even = product("fm,mo->fo", taps_even, kernel_one) + small_params[14]
    pre_odd = product("fm,mo->fo", taps_odd, kernel_one) + small_params[14]
    odd_open = jnp.logical_or(
        part_index > 0, jnp.arange(enc_rows + 1, dtype=jnp.int32) > 0
    )[:, None]
    first_even = to_low(gelu_exact(pre_even))
    first_odd = to_low(jnp.where(odd_open, gelu_exact(pre_odd), 0.0))
    first_even, first_odd, held_of[3], teach_weight = together(
        first_even, first_odd, held_of[3], teach_weight
    )
    unpack(groups[3], plane_full(held_of[3]))
    taps_two = (first_odd[:-1], first_even, first_odd[1:])
    second_pre = small_params[15]
    for tap in range(KW):
        second_pre = second_pre + product("ji,oi->jo", taps_two[tap], conv_full[tap])
    stream_zero = gelu_exact(second_pre) + sinusoid(part_index * enc_rows, enc_rows, D)
    enc_one = to_low(layer_norm(stream_zero, small_params[0], small_params[1]))
    enc_one, table_held = together(enc_one, table_held)
    table_block = lax.all_gather(table_held, "fsdp", axis=0, tiled=True)
    enc_one_clip = spread_rows(enc_one)
    enc_weights = (narrow_full[0], narrow_full[1], narrow_full[2], narrow_full[9])
    attn_out, enc_saved = attention_forward(
        enc_one,
        enc_one_clip,
        enc_weights,
        (small_params[16], small_params[17], small_params[18]),
        None,
        None,
    )
    stream_one = stream_zero + attn_out
    enc_two = to_low(layer_norm(stream_one, small_params[2], small_params[3]))
    feed_out, enc_feed_saved = feed_forward_pass(
        enc_two, feed_full[0], hidden_bias[0], feed_full[1], small_params[19]
    )
    stream_two = stream_one + feed_out
    encoded = to_low(layer_norm(stream_two, small_params[4], small_params[5]))
    encoded_clip = spread_rows(encoded)

    dec_start = part_index * dec_rows
    query_place = dec_start + row_place
    if paired:
        key_place = jnp.concatenate([query_place, (1 - part_index) * dec_rows + row_place])
    else:
        key_place = jnp.arange(dec_rows * part_count, dtype=jnp.int32)
    position_start = NVEC + KW * MEL
    tokens_zero = embedded + lax.dynamic_slice_in_dim(
        small_params, position_start + dec_start, dec_rows, 0
    )
    dec_one = to_low(layer_norm(tokens_zero, small_params[6], small_params[7]))
    dec_one_clip = spread_rows(dec_one)
    self_weights = (narrow_full[3], narrow_full[4], narrow_full[5], narrow_full[10])
    self_out, self_saved = attention_forward(
        dec_one,
        dec_one_clip,
        self_weights,
        (small_params[20], small_params[21], small_params[22]),
        key_place,
        query_place,
    )
    tokens_one = tokens_zero + self_out
    dec_two = to_low(layer_norm(tokens_one, small_params[8], small_params[9]))
    cross_weights = (narrow_full[6], narrow_full[7], narrow_full[8], narrow_full[11])
    cross_out, cross_saved = attention_forward(
        dec_two,
        encoded_clip,
        cross_weights,
        (small_params[23], small_params[24], small_params[25]),
        None,
        None,
    )
    tokens_two = tokens_one + cross_out
    dec_three = to_low(layer_norm(tokens_two, small_params[10], small_params[11]))
    dec_feed_out, dec_feed_saved = feed_forward_pass(
        dec_three, feed_full[2], hidden_bias[1], feed_full[3], small_params[26]
    )
    tokens_three = tokens_two + dec_feed_out
    tokens_three, table_block = together(tokens_three, table_block)
    final = to_low(layer_norm(tokens_three, small_params[12], small_params[13]))

    moved_own = pick(moved, block_index).astype(jnp.bfloat16)
    final_moved = to_low(product("np,pd->nd", moved_own, final))
    final_all = lax.all_gather(final_moved, PLANE, axis=0, tiled=True)
    top_lanes, total_lanes, picked, dots = loss_stats(
        final_all, table_block, bias_row, target_local, teach_weight, blocks
    )
    top_own = jnp.max(top_lanes, axis=1)
    total_own = jnp.sum(total_lanes * jnp.exp(top_lanes - top_own[:, None]), axis=1)
    stats = lax.all_gather(jnp.stack([top_own, total_own]), PLANE, axis=0)
    joint_top = jnp.max(stats[:, 0], axis=0)
    joint_total = jnp.sum(stats[:, 1] * jnp.exp(stats[:, 0] - joint_top), axis=0)
    log_total = joint_top + jnp.log(joint_total)
    loss_term = (
        jnp.sum(row_weight * log_total) / blocks
        + jnp.sum(teach_probs * jnp.log(teach_probs)) / (teach_total * tp_count)
        - jnp.sum(picked) * token_share
        - jnp.sum(dots)
    )
    levels = (log_total - jnp.log(row_weight))[:, None]
    final_grad, table_grad = loss_grads(
        final_all, table_block, bias_row, target_local, levels, teach_weight, blocks, token_share
    )
    grad_final_moved = lax.psum_scatter(
        to_low(final_grad), PLANE, scatter_dimension=0, tiled=True
    )
    grad_final = product("np,nd->pd", moved_own, grad_final_moved)

    table_sum = lax.psum_scatter(table_grad, "fsdp", scatter_dimension=0, tiled=True)

    def cut_narrow(grad, height):
        return (
            to_low(grad)
            .reshape(fsdp_count, ctx_count, tp_count, height, D)
            .transpose(1, 2, 0, 3, 4)
        )

    def cut_feed(grad):
        return (
            to_low(grad)
            .reshape(fsdp_count, ctx_count, thick, tp_count, D)
            .transpose(1, 3, 0, 2, 4)
        )

    def packed_grads(pieces):
        held = jnp.concatenate(pieces, axis=3)
        return held.reshape((blocks,) + held.shape[2:])

    def plane_sum(held):
        return lax.psum_scatter(held, PLANE, scatter_dimension=0, tiled=False)

    def own_columns(grad, heights):
        cut = to_low(grad).reshape(grad.shape[0], tp_count, D // tp_count).swapaxes(0, 1)
        arrived = lax.all_to_all(cut, "tp", 0, 0, tiled=True).astype(jnp.float32)
        out, offset = [], 0
        for height in heights:
            out.append(
                arrived[:, offset : offset + height].reshape(
                    tp_count * height, D // tp_count
                )
            )
            offset += height
        return out

    row_grads = {}
    grad_three, row_grads[12], row_grads[13] = norm_back(
        tokens_three, small_params[12], small_params[13], grad_final
    )
    grad_feed = to_low(grad_three)
    row_grads[26] = jnp.sum(grad_feed, axis=0, dtype=jnp.float32)
    feed_grad_2, feed_grad_3, dec_bias_in, back = feed_backward(
        dec_three, feed_full[2], feed_full[3], dec_feed_saved, grad_feed
    )
    held_dec_feed = packed_grads([cut_feed(feed_grad_2), cut_feed(feed_grad_3)])
    back, held_dec_feed = together(back, held_dec_feed)
    part_dec_feed = plane_sum(held_dec_feed)
    back, row_grads[10], row_grads[11] = norm_back(
        tokens_two, small_params[10], small_params[11], back
    )
    grad_two = grad_three + back
    grad_cross = to_low(grad_two)
    row_grads[25] = jnp.sum(grad_cross, axis=0, dtype=jnp.float32)
    cross_grads, row_grads[23], row_grads[24], back_q, back_encoded = attention_backward(
        dec_two, encoded_clip, cross_weights, cross_saved, grad_cross, None, None
    )
    back, row_grads[8], row_grads[9] = norm_back(
        tokens_one, small_params[8], small_params[9], back_q
    )
    grad_one = grad_two + back
    grad_self = to_low(grad_one)
    row_grads[22] = jnp.sum(grad_self, axis=0, dtype=jnp.float32)
    self_grads, row_grads[20], row_grads[21], back_q, back_k = attention_backward(
        dec_one, dec_one_clip, self_weights, self_saved, grad_self, key_place, query_place
    )
    held_dec_attn = packed_grads([cut_narrow(grad, piece) for grad in self_grads + cross_grads])
    back, row_grads[6], row_grads[7] = norm_back(
        tokens_zero, small_params[6], small_params[7], back_q + collect_rows(back_k)
    )
    grad_zero = grad_one + back
    position_rows = lax.dynamic_update_slice_in_dim(
        jnp.zeros((dec_rows * part_count, D), jnp.float32), grad_zero, dec_start, 0
    )
    sent = to_low(grad_zero).reshape(dec_rows, fsdp_count * ctx_count, thick).swapaxes(0, 1)
    sent = lax.all_to_all(sent, ("fsdp", "ctx"), 0, 0, tiled=True)
    sent = sent.reshape(fsdp_count, ctx_count, dec_rows, thick)
    sent = lax.all_gather(sent, "tp", axis=0).reshape(-1, thick).astype(jnp.float32)
    embed_grad = scatter_add(jnp.where(ids_inside, ids_local, vocab_local), sent, vocab_local)

    def small_plane_sum(rows):
        rows = jnp.pad(rows, ((0, -rows.shape[0] % (8 * blocks)), (0, 0)))
        return lax.psum_scatter(rows, PLANE, scatter_dimension=0, tiled=True)

    position_part = small_plane_sum(position_rows)

    back_encoded, held_dec_attn, table_sum = together(back_encoded, held_dec_attn, table_sum)
    part_dec_attn = plane_sum(held_dec_attn)
    back_encoded_own = collect_rows(back_encoded)
    grad_stream_two, row_grads[4], row_grads[5] = norm_back(
        stream_two, small_params[4], small_params[5], back_encoded_own
    )
    grad_feed = to_low(grad_stream_two)
    row_grads[19] = jnp.sum(grad_feed, axis=0, dtype=jnp.float32)
    feed_grad_0, feed_grad_1, enc_bias_in, back = feed_backward(
        enc_two, feed_full[0], feed_full[1], enc_feed_saved, grad_feed
    )
    held_enc_feed = packed_grads([cut_feed(feed_grad_0), cut_feed(feed_grad_1)])
    back, row_grads[2], row_grads[3] = norm_back(
        stream_one, small_params[2], small_params[3], back
    )
    grad_stream_one = grad_stream_two + back
    grad_stream_one, part_dec_feed, held_enc_feed = together(
        grad_stream_one, part_dec_feed, held_enc_feed
    )
    part_enc_feed = plane_sum(held_enc_feed)
    sum_dec_feed = sum_to_owner(part_dec_feed, "fsdp")
    grad_attn = to_low(grad_stream_one)
    row_grads[18] = jnp.sum(grad_attn, axis=0, dtype=jnp.float32)
    enc_grads, row_grads[16], row_grads[17], back_q, back_k = attention_backward(
        enc_one, enc_one_clip, enc_weights, enc_saved, grad_attn, None, None
    )
    back, row_grads[0], row_grads[1] = norm_back(
        stream_zero, small_params[0], small_params[1], back_q + collect_rows(back_k)
    )
    grad_stream_zero = grad_stream_one + back
    grad_stream_zero, part_dec_attn, position_part, sum_dec_feed = together(
        grad_stream_zero, part_dec_attn, position_part, sum_dec_feed
    )
    sum_dec_attn = sum_to_owner(part_dec_attn, "fsdp")
    position_part = exchanged_sum(position_part, ("fsdp",))
    table_sum = table_sum.reshape(ctx_count, thick, vocab_part)
    table_sum = in_order(
        sent_to_owners(lambda step: pick(table_sum, lax.rem(ctx_index + step, ctx_count)), "ctx"),
        "ctx",
    )
    table_sum = table_sum.swapaxes(0, 1).reshape(thick, ctx_count * vocab_part)[:, :vocab_local]
    grad_second = to_low(gelu_back(second_pre, grad_stream_zero))
    row_grads[15] = jnp.sum(grad_second, axis=0, dtype=jnp.float32)
    conv_grads = [product("jo,ji->oi", grad_second, taps_two[tap]) for tap in range(KW)]
    held_enc_attn = packed_grads(
        [cut_narrow(jnp.concatenate(conv_grads, axis=0), KW * piece)]
        + [cut_narrow(grad, piece) for grad in enc_grads]
    )
    sum_enc_attn = sum_to_owner(plane_sum(held_enc_attn), "fsdp")
    sum_enc_feed = sum_to_owner(part_enc_feed, "fsdp")
    grad_taps = [product("jo,oi->ji", grad_second, conv_full[tap]) for tap in range(KW)]
    grad_odd = jnp.pad(grad_taps[0], ((0, 1), (0, 0))) + jnp.pad(grad_taps[2], ((1, 0), (0, 0)))
    grad_pre_even = to_low(gelu_back(pre_even, grad_taps[1]))
    grad_pre_odd = to_low(jnp.where(odd_open, gelu_back(pre_odd, grad_odd), 0.0))
    row_grads[14] = jnp.sum(grad_pre_even, axis=0, dtype=jnp.float32) + jnp.sum(
        grad_pre_odd, axis=0, dtype=jnp.float32
    )
    kernel_rows = product("fm,fo->mo", taps_even, grad_pre_even) + product(
        "fm,fo->mo", taps_odd, grad_pre_odd
    )

    vector_rows = jnp.concatenate(
        [
            jnp.stack([row_grads[row] for row in range(27)]),
            enc_bias_in.reshape(4, D),
            dec_bias_in.reshape(4, D),
            kernel_rows,
        ]
    )
    vector_part = exchanged_sum(small_plane_sum(vector_rows), ("fsdp",))
    all_small = lax.all_gather(jnp.concatenate([vector_part, position_part]), PLANE, axis=0)
    split = vector_part.shape[0]
    small_grad = jnp.concatenate(
        [
            all_small[:, :split].reshape(-1, D)[: vector_rows.shape[0]],
            all_small[:, split:].reshape(-1, D)[: position_rows.shape[0]],
        ]
    )

    (embed_flat,) = together(embed_grad.T)
    shard_table = table_sum.astype(jnp.float32) + embed_flat
    dec_list = own_columns(sum_dec_attn, (piece,) * 8)
    enc_list = own_columns(sum_enc_attn, (KW * piece,) + (piece,) * 4)
    shard_conv = enc_list[0]
    shard_proj = jnp.stack(enc_list[1:4] + dec_list[0:3] + dec_list[4:7])
    shard_out = jnp.stack([enc_list[4], dec_list[3], dec_list[7]])
    shard_feed = jnp.concatenate([sum_enc_feed, sum_dec_feed]).reshape(4, thick, D)
    local_squares = (
        jnp.sum(shard_proj * shard_proj)
        + jnp.sum(shard_out * shard_out)
        + jnp.sum(shard_feed * shard_feed)
        + jnp.sum(shard_conv * shard_conv)
        + jnp.sum(shard_table * shard_table)
    )
    loss_value, big_squares = exchanged_sum(jnp.stack([loss_term, local_squares]), ALL)
    grad_norm = jnp.sqrt(big_squares + jnp.sum(small_grad * small_grad))
    factor = jnp.minimum(1.0, CLIP_NORM / (grad_norm + 1e-06))
    results = [
        nesterov(projections, shard_proj, moment_projections, average_projections, factor),
        nesterov(out_proj, shard_out, moment_out_proj, average_out_proj, factor),
        nesterov(feed_forward, shard_feed, moment_feed_forward, average_feed_forward, factor),
        nesterov(conv_kernels, shard_conv, moment_conv_kernels, average_conv_kernels, factor),
        tuple(
            part.T
            for part in nesterov(
                embed_table.T, shard_table, moment_embed_table.T, average_embed_table.T, factor
            )
        ),
        nesterov(small_params, small_grad, moment_small_params, average_small_params, factor),
    ]
    return (loss_value, grad_norm) + tuple(
        result[kind] for kind in range(3) for result in results
    )


def solution(mesh):
    by_rows = P(None, ("fsdp", "ctx"), "tp")
    weights = (
        by_rows,
        by_rows,
        by_rows,
        P(("fsdp", "ctx"), "tp"),
        P("tp", ("fsdp", "ctx")),
        P(),
    )
    pair = P("fsdp", "ctx")
    wide = P("fsdp", "ctx", None)
    in_specs = (wide, pair, pair, pair, wide, wide, P("tp")) + 3 * weights
    out_specs = (P(), P()) + 3 * weights
    return jax.shard_map(local, mesh=mesh, in_specs=in_specs, out_specs=out_specs, check_vma=False)
```

```python
import functools
import math

import jax
import jax.numpy as jnp
from jax import lax
from jax.experimental import pallas as pl
from jax.experimental.pallas import tpu as pltpu
from jax.sharding import PartitionSpec as P

D = 768
H = 12
HD = 64
FF = 3072
MEL = 80
KW = 3
NVEC = 35
EPSILON = 1e-05
CLIP_NORM = 1.0
MOMENTUM = 0.9
LEARN_RATE = 20.0
AVERAGE_RATE = 0.1
NEG_FILL = -1e30
CHUNK = 512
LANES = 128
VMEM_LIMIT = 56 * 1024 * 1024
PLANE = ("ctx", "tp")
ALL = ("fsdp", "ctx", "tp")


def to_low(values):
    return values.astype(jnp.bfloat16)


def product(pattern, left, right):
    return jnp.einsum(pattern, left, right, preferred_element_type=jnp.float32)


def layer_norm(values, scale_row, shift_row):
    center = values - jnp.mean(values, axis=-1, keepdims=True)
    spread = jnp.mean(center * center, axis=-1, keepdims=True)
    return center * lax.rsqrt(spread + EPSILON) * scale_row + shift_row


def norm_back(values, scale_row, shift_row, upstream):
    unused_out, pullback = jax.vjp(layer_norm, values, scale_row, shift_row)
    return pullback(upstream)


def gelu_exact(values):
    return jax.nn.gelu(values, approximate=False)


def gelu_back(values, upstream):
    unused_out, pullback = jax.vjp(gelu_exact, values)
    return pullback(upstream)[0]


def sinusoid(start, count, width):
    half_width = width // 2
    increment = math.log(10000.0) / (half_width - 1)
    inverse = jnp.exp(-increment * jnp.arange(half_width, dtype=jnp.int32).astype(jnp.float32))
    moments = (start + jnp.arange(count, dtype=jnp.int32)).astype(jnp.float32)
    angles = moments[:, None] * inverse[None, :]
    return jnp.concatenate([jnp.sin(angles), jnp.cos(angles)], axis=1)


def pick(values, index):
    return lax.dynamic_index_in_dim(values, index, 0, keepdims=False)


def place(values, part, index):
    return lax.dynamic_update_index_in_dim(values, part, index, 0)


def shifted(axis, step):
    count = lax.axis_size(axis)
    return [(i, (i + step) % count) for i in range(count)]


def in_order(arrived, axis):
    count = len(arrived)
    index = lax.axis_index(axis)
    if count == 2:
        return jnp.where(index == 0, jnp.stack(arrived), jnp.stack(arrived[::-1]))
    out = jnp.zeros((count,) + arrived[0].shape, arrived[0].dtype)
    for step, piece in enumerate(arrived):
        out = place(out, piece, lax.rem(index - step + count, count))
    return out


def sent_to_all(values, axis):
    count = lax.axis_size(axis)
    return [values] + [
        lax.ppermute(values, axis, shifted(axis, step)) for step in range(1, count)
    ]


def spread(values, axis):
    return in_order(sent_to_all(values, axis), axis)


def sent_to_owners(pieces_for, axis):
    count = lax.axis_size(axis)
    return [pieces_for(0)] + [
        lax.ppermute(pieces_for(step), axis, shifted(axis, step)) for step in range(1, count)
    ]


def wide_sum(pieces):
    total = pieces[0].astype(jnp.float32)
    for piece in pieces[1:]:
        total = total + piece.astype(jnp.float32)
    return total


def sum_to_owner(values, axis):
    count = lax.axis_size(axis)
    index = lax.axis_index(axis)
    return wide_sum(
        sent_to_owners(lambda step: pick(values, lax.rem(index + step, count)), axis)
    )


def together(*values):
    return lax.optimization_barrier(values)


def exchanged_sum(values, axes):
    for axis in axes:
        count = lax.axis_size(axis)
        if count == 4:
            at = sent_to_all(values, axis)
            values = (at[0] + at[2]) + (at[1] + at[3])
            continue
        bit = 1
        while bit < count:
            values = values + lax.ppermute(values, axis, [(i, i ^ bit) for i in range(count)])
            bit *= 2
    return values


def head_scores(queries, keys, key_place, query_place):
    scores = product("qhd,khd->hqk", queries, keys) * HD ** (-0.5)
    if key_place is not None:
        allowed = key_place[None, :] <= query_place[:, None]
        scores = jnp.where(allowed[None], scores, NEG_FILL)
    return scores


def split_heads(values):
    return values.reshape(values.shape[0], H, HD)


def attention_forward(rows_q, rows_k, weights, biases, key_place, query_place):
    queries = split_heads(to_low(product("qd,dh->qh", rows_q, weights[0]) + biases[0]))
    keys = split_heads(to_low(product("qd,dh->qh", rows_k, weights[1])))
    values = split_heads(to_low(product("qd,dh->qh", rows_k, weights[2]) + biases[1]))
    scores = head_scores(queries, keys, key_place, query_place)
    top = jnp.max(scores, axis=-1, keepdims=True)
    raised = jnp.exp(scores - top)
    total = jnp.sum(raised, axis=-1, keepdims=True)
    mixed = product("hqk,khd->qhd", to_low(raised / total), values)
    mixed = to_low(mixed.reshape(rows_q.shape))
    out = product("qh,oh->qo", mixed, weights[3]) + biases[2]
    return out, (queries, keys, values, mixed, top + jnp.log(total))


def attention_backward(rows_q, rows_k, weights, saved, grad_out, key_place, query_place):
    queries, keys, values, mixed, log_total = saved
    grad_out_weight = product("qo,qh->oh", grad_out, mixed)
    grad_mixed = split_heads(to_low(product("qo,oh->qh", grad_out, weights[3])))
    scores = head_scores(queries, keys, key_place, query_place)
    probs = jnp.exp(scores - log_total)
    grad_probs = product("qhd,khd->hqk", grad_mixed, values)
    inner = jnp.sum(probs * grad_probs, axis=-1, keepdims=True)
    grad_scores = to_low(probs * (grad_probs - inner))
    factor = HD ** (-0.5)
    grad_q = to_low(product("hqk,khd->qhd", grad_scores, keys) * factor).reshape(rows_q.shape)
    grad_k = to_low(product("hqk,qhd->khd", grad_scores, queries) * factor).reshape(rows_k.shape)
    grad_v = to_low(product("hqk,qhd->khd", to_low(probs), grad_mixed)).reshape(rows_k.shape)
    grad_weights = (
        product("qd,qh->dh", rows_q, grad_q),
        product("qd,qh->dh", rows_k, grad_k),
        product("qd,qh->dh", rows_k, grad_v),
        grad_out_weight,
    )
    bias_q = jnp.sum(grad_q, axis=0, dtype=jnp.float32)
    bias_v = jnp.sum(grad_v, axis=0, dtype=jnp.float32)
    back_q = product("qh,dh->qd", grad_q, weights[0])
    back_k = product("qh,dh->qd", grad_k, weights[1]) + product("qh,dh->qd", grad_v, weights[2])
    return grad_weights, bias_q, bias_v, back_q, back_k


def feed_forward_pass(rows, weight_in, bias_in, weight_out, bias_out):
    hidden = product("qd,df->qf", rows, weight_in) + bias_in
    active = to_low(gelu_exact(hidden))
    return product("qf,of->qo", active, weight_out) + bias_out, (hidden, active)


def feed_backward(rows, weight_in, weight_out, saved, grad_out):
    hidden, active = saved
    grad_weight_out = product("qo,qf->of", grad_out, active)
    grad_active = product("qo,of->qf", grad_out, weight_out)
    grad_hidden = to_low(gelu_back(hidden, grad_active))
    grad_weight_in = product("qd,qf->df", rows, grad_hidden)
    grad_bias_in = jnp.sum(grad_hidden, axis=0, dtype=jnp.float32)
    back = product("qf,df->qd", grad_hidden, weight_in)
    return grad_weight_in, grad_weight_out, grad_bias_in, back


def nesterov(weight, grad, moment, average, factor):
    clipped = grad * factor
    moment_new = MOMENTUM * moment + clipped
    change = -LEARN_RATE * (clipped + MOMENTUM * moment_new)
    average_new = average + AVERAGE_RATE * (weight + change - average)
    return (change, moment_new, average_new)


def stats_kernel(
    blocks, rows, teach, final_ref, bias_ref, target_ref, weight_ref, table_ref,
    top_ref, total_ref, pick_ref, dot_ref,
):
    chunk = table_ref.shape[1]
    tiles = chunk // LANES

    @pl.when(pl.program_id(0) == 0)
    def _():
        top_ref[...] = jnp.full(top_ref.shape, 2.0 * NEG_FILL, jnp.float32)
        total_ref[...] = jnp.zeros(total_ref.shape, jnp.float32)
        pick_ref[...] = jnp.zeros(pick_ref.shape, jnp.float32)
        dot_ref[...] = jnp.zeros(dot_ref.shape, jnp.float32)

    start = pl.program_id(0) * chunk
    for block in range(blocks):
        span = pl.ds(block * rows, rows)
        logits = jnp.dot(final_ref[span, :], table_ref[...], preferred_element_type=jnp.float32)
        target = target_ref[span, :] - start
        top_old = top_ref[span, :]
        masked = []
        picked = pick_ref[span, :]
        top_new = top_old
        dots = dot_ref[...]
        for tile in range(tiles):
            lanes = slice(tile * LANES, (tile + 1) * LANES)
            piece = logits[:, lanes]
            column = lax.broadcasted_iota(jnp.int32, (rows, LANES), 1) + tile * LANES
            picked = picked + jnp.where(column == target, piece, 0.0)
            dots = dots + piece[:teach] * weight_ref[
                tile, pl.ds(block * teach, teach), :
            ].astype(jnp.float32)
            piece = piece + bias_ref[:, lanes]
            masked.append(piece)
            top_new = jnp.maximum(top_new, piece)
        total = total_ref[span, :] * jnp.exp(top_old - top_new)
        for piece in masked:
            total = total + jnp.exp(piece - top_new)
        top_ref[span, :] = top_new
        total_ref[span, :] = total
        pick_ref[span, :] = picked
        dot_ref[...] = dots


def loss_stats(final_all, table, bias_row, targets, weights, blocks):
    count = final_all.shape[0]
    width = table.shape[1]
    rows = count // blocks
    teach = weights.shape[1] // blocks
    whole = lambda j: (0, 0)
    by_chunk = lambda j: (0, j)
    row_stat = jax.ShapeDtypeStruct((count, LANES), jnp.float32)
    return pl.pallas_call(
        functools.partial(stats_kernel, blocks, rows, teach),
        grid=(width // CHUNK,),
        in_specs=[
            pl.BlockSpec((count, D), whole),
            pl.BlockSpec((1, CHUNK), by_chunk),
            pl.BlockSpec((count, 1), whole),
            pl.BlockSpec((CHUNK // LANES, weights.shape[1], LANES), lambda j: (j, 0, 0)),
            pl.BlockSpec((D, CHUNK), by_chunk),
        ],
        out_specs=[
            pl.BlockSpec((count, LANES), whole),
            pl.BlockSpec((count, LANES), whole),
            pl.BlockSpec((count, LANES), whole),
            pl.BlockSpec((teach, LANES), whole),
        ],
        out_shape=[
            row_stat,
            row_stat,
            row_stat,
            jax.ShapeDtypeStruct((teach, LANES), jnp.float32),
        ],
        compiler_params=pltpu.CompilerParams(
            vmem_limit_bytes=VMEM_LIMIT, dimension_semantics=("arbitrary",)
        ),
        cost_estimate=pl.CostEstimate(
            flops=2 * count * D * width,
            bytes_accessed=2 * (D + weights.shape[1]) * width,
            transcendentals=count * width,
        ),
        name="loss_stats",
    )(final_all, bias_row, targets, weights, table)


def grads_kernel(
    blocks, rows, teach, token_share, final_ref, flipped_ref, bias_ref, target_ref, level_ref,
    weight_ref, table_ref, final_low_ref, table_grad_ref, low_ref, final_grad_ref,
):
    chunk = table_ref.shape[1]
    start = pl.program_id(0) * chunk

    @pl.when(pl.program_id(0) == 0)
    def _():
        final_grad_ref[...] = jnp.zeros(final_grad_ref.shape, jnp.float32)

    for block in range(blocks):
        span = pl.ds(block * rows, rows)
        logits = jnp.dot(final_ref[span, :], table_ref[...], preferred_element_type=jnp.float32)
        column = lax.broadcasted_iota(jnp.int32, (rows, chunk), 1)
        target = target_ref[span, :] - start
        grad = jnp.exp(logits + bias_ref[...] - level_ref[span, :])
        grad = grad - jnp.where(column == target, token_share, 0.0)
        for tile in range(chunk // LANES):
            lanes = slice(tile * LANES, (tile + 1) * LANES)
            weight = weight_ref[tile, pl.ds(block * teach, teach), :].astype(jnp.float32)
            low_ref[pl.ds(block * rows, teach), lanes] = to_low(grad[:teach, lanes] - weight)
        low_ref[pl.ds(block * rows + teach, rows - teach), :] = to_low(grad[teach:])
        final_grad_ref[span, :] += lax.dot_general(
            low_ref[span, :],
            table_ref[...],
            (((1,), (1,)), ((), ())),
            preferred_element_type=jnp.float32,
        )
    table_grad_ref[...] = to_low(
        jnp.dot(flipped_ref[...], low_ref[...], preferred_element_type=jnp.float32)
    )

    @pl.when(pl.program_id(0) == pl.num_programs(0) - 1)
    def _():
        final_low_ref[...] = to_low(final_grad_ref[...])


def loss_grads(final_all, table, bias_row, targets, levels, weights, blocks, token_share):
    count = final_all.shape[0]
    width = table.shape[1]
    rows = count // blocks
    teach = weights.shape[1] // blocks
    whole = lambda j: (0, 0)
    by_chunk = lambda j: (0, j)
    return pl.pallas_call(
        functools.partial(grads_kernel, blocks, rows, teach, token_share),
        grid=(width // CHUNK,),
        in_specs=[
            pl.BlockSpec((count, D), whole),
            pl.BlockSpec((D, count), whole),
            pl.BlockSpec((1, CHUNK), by_chunk),
            pl.BlockSpec((count, 1), whole),
            pl.BlockSpec((count, 1), whole),
            pl.BlockSpec((CHUNK // LANES, weights.shape[1], LANES), lambda j: (j, 0, 0)),
            pl.BlockSpec((D, CHUNK), by_chunk),
        ],
        out_specs=[pl.BlockSpec((count, D), whole), pl.BlockSpec((D, CHUNK), by_chunk)],
        out_shape=[
            jax.ShapeDtypeStruct((count, D), jnp.bfloat16),
            jax.ShapeDtypeStruct((D, width), jnp.bfloat16),
        ],
        scratch_shapes=[
            pltpu.VMEM((count, CHUNK), jnp.bfloat16),
            pltpu.VMEM((count, D), jnp.float32),
        ],
        compiler_params=pltpu.CompilerParams(
            vmem_limit_bytes=VMEM_LIMIT, dimension_semantics=("arbitrary",)
        ),
        cost_estimate=pl.CostEstimate(
            flops=6 * count * D * width,
            bytes_accessed=2 * (2 * D + weights.shape[1]) * width + 4 * count * D,
            transcendentals=count * width,
        ),
        name="loss_grads",
    )(final_all, final_all.T, bias_row, targets, levels, weights, table)


def lookup_kernel(place_ref, table_ref, out_ref):
    def some(group, carry):
        for at in range(16):
            row = group * 16 + at
            out_ref[pl.ds(row, 1), :] = table_ref[pl.ds(place_ref[row], 1), :]
        return carry

    lax.fori_loop(0, out_ref.shape[0] // 16, some, 0)


def lookup(places, table):
    count, width = places.shape[0], table.shape[1]
    return pl.pallas_call(
        lookup_kernel,
        out_shape=jax.ShapeDtypeStruct((count, width), jnp.float32),
        in_specs=[
            pl.BlockSpec(memory_space=pltpu.SMEM),
            pl.BlockSpec(memory_space=pltpu.VMEM),
        ],
        out_specs=pl.BlockSpec(memory_space=pltpu.VMEM),
        compiler_params=pltpu.CompilerParams(vmem_limit_bytes=VMEM_LIMIT),
        cost_estimate=pl.CostEstimate(
            flops=count * width, bytes_accessed=70_000_000, transcendentals=0
        ),
        name="lookup",
    )(places, table)


def scatter_kernel(place_ref, grad_ref, out_ref, *sum_refs):
    streams = len(sum_refs)
    width = grad_ref.shape[1]
    for sum_ref in sum_refs:
        sum_ref[...] = jnp.zeros(sum_ref.shape, jnp.float32)
    run = grad_ref.shape[0] // streams

    def some(group, carry):
        for at in range(4):
            for stream, sum_ref in enumerate(sum_refs):
                row = stream * run + group * 4 + at
                sum_ref[pl.ds(place_ref[row], 1), :width] += grad_ref[pl.ds(row, 1), :]
        return carry

    lax.fori_loop(0, run // 4, some, 0)

    def turn(block, carry):
        span = pl.ds(pl.multiple_of(block * LANES, LANES), LANES)
        total = sum_refs[0][span, :]
        for sum_ref in sum_refs[1:]:
            total = total + sum_ref[span, :]
        out_ref[:, span] = total.T[:width]
        return carry

    lax.fori_loop(0, out_ref.shape[1] // LANES, turn, 0)


def scatter_add(places, grads, height):
    count, width = grads.shape
    padded = (height // LANES + 1) * LANES
    out = pl.pallas_call(
        scatter_kernel,
        out_shape=jax.ShapeDtypeStruct((width, padded), jnp.float32),
        in_specs=[
            pl.BlockSpec(memory_space=pltpu.SMEM),
            pl.BlockSpec(memory_space=pltpu.VMEM),
        ],
        out_specs=pl.BlockSpec(memory_space=pltpu.VMEM),
        scratch_shapes=[pltpu.VMEM((padded, LANES), jnp.float32)] * 4,
        compiler_params=pltpu.CompilerParams(vmem_limit_bytes=VMEM_LIMIT),
        cost_estimate=pl.CostEstimate(
            flops=count * width, bytes_accessed=90_000_000, transcendentals=0
        ),
        name="scatter_add",
    )(places, grads)
    return out[:, :height]


def local(
    mel_frames,
    dec_ids,
    targets,
    teach_rows,
    teach_ids,
    teach_probs,
    vocab_mask,
    projections,
    out_proj,
    feed_forward,
    conv_kernels,
    embed_table,
    small_params,
    moment_projections,
    moment_out_proj,
    moment_feed_forward,
    moment_conv_kernels,
    moment_embed_table,
    moment_small_params,
    average_projections,
    average_out_proj,
    average_feed_forward,
    average_conv_kernels,
    average_embed_table,
    average_small_params,
):
    fsdp_count, ctx_count, tp_count = (lax.axis_size(axis) for axis in ALL)
    fsdp_index, ctx_index, tp_index = (lax.axis_index(axis) for axis in ALL)
    clip_count = mel_frames.shape[0]
    blocks = ctx_count * tp_count
    part_count = ctx_count
    paired = ctx_count == 2 and tp_count % 2 == 0
    block_index = ctx_index * tp_count + tp_index
    if paired:
        clip_index, part_index = block_index // 2, block_index % 2
        part_of_block = jnp.arange(blocks, dtype=jnp.int32) % 2
    else:
        clip_index, part_index = tp_index, ctx_index
        part_of_block = jnp.arange(blocks, dtype=jnp.int32) // tp_count

    def in_blocks(values):
        if paired:
            values = jnp.swapaxes(values, 0, 1)
        return values.reshape((blocks,) + values.shape[2:])

    pairs = [(i, i ^ 1) for i in range(tp_count)]

    def spread_rows(rows):
        if paired:
            return jnp.concatenate([rows, lax.ppermute(rows, "tp", pairs)], axis=0)
        return lax.all_gather(rows, "ctx", axis=0, tiled=True)

    def collect_rows(rows):
        if paired:
            half = rows.shape[0] // 2
            other = lax.ppermute(to_low(rows[half:]), "tp", pairs)
            return rows[:half] + other.astype(jnp.float32)
        return lax.psum_scatter(to_low(rows), "ctx", scatter_dimension=0, tiled=True).astype(
            jnp.float32
        )

    enc_rows = mel_frames.shape[1] // 2
    dec_rows = dec_ids.shape[1]
    teach_count = teach_rows.shape[1]
    vocab_local = embed_table.shape[0]

    piece = D // (fsdp_count * ctx_count * tp_count)
    thick = D // (fsdp_count * ctx_count)

    def by_owner(values):
        count, height, width = values.shape
        return values.reshape(count, tp_count, height // tp_count, width).swapaxes(0, 1)

    def swapped_rows(values):
        arrived = lax.all_to_all(values, "tp", 0, 0, tiled=True)
        return arrived.transpose(1, 2, 0, 3).reshape(arrived.shape[1], arrived.shape[2], D)

    narrow_attn = by_owner(jnp.concatenate([to_low(projections), to_low(out_proj)], axis=0))
    narrow_conv = by_owner(to_low(conv_kernels)[None])
    narrow_conv = narrow_conv.reshape(tp_count, KW, piece, D // tp_count)
    own_rows = swapped_rows(jnp.concatenate([narrow_attn, narrow_conv], axis=1))
    feed_low = to_low(feed_forward)

    groups = (
        ((0, 1, 2, 9), (), True),
        ((), (0, 1), False),
        ((3, 4, 5, 10, 6, 7, 8, 11), (), False),
        ((), (2, 3), False),
    )
    narrow_full, feed_full = {}, {}
    stacks = []
    for narrow_members, feed_members, with_conv in groups:
        parts = []
        if with_conv:
            parts.append(own_rows[12:].reshape(KW * piece, D))
        parts += [own_rows[member] for member in narrow_members]
        parts += [feed_low[member] for member in feed_members]
        stacks.append(jnp.concatenate(parts, axis=0))
    held_of = [spread(stack, "fsdp") for stack in stacks]

    def plane_full(held):
        return lax.all_gather(held, PLANE, axis=0).reshape(
            (ctx_count, tp_count) + held.shape
        )

    def unpack(group, full):
        narrow_members, feed_members, with_conv = group
        offset = KW * piece if with_conv else 0
        for member in narrow_members:
            narrow_full[member] = (
                full[:, :, :, offset : offset + piece].transpose(2, 0, 1, 3, 4).reshape(D, D)
            )
            offset += piece
        for member in feed_members:
            feed_full[member] = (
                full[:, :, :, offset : offset + thick].transpose(2, 0, 3, 1, 4).reshape(D, FF)
            )
            offset += thick

    vocab_part = -(-vocab_local // (ctx_count * CHUNK)) * CHUNK
    table_low = to_low(embed_table)
    table_wide = jnp.pad(table_low.T, ((0, 0), (0, ctx_count * vocab_part - vocab_local)))

    def vocab_slice(step):
        start = lax.rem(ctx_index + step, ctx_count) * vocab_part
        return lax.dynamic_slice_in_dim(table_wide, start, vocab_part, 1)

    table_held = in_order(sent_to_owners(vocab_slice, "ctx"), "ctx")
    table_held = table_held.reshape(ctx_count * thick, vocab_part)

    held_of[0], dec_ids = together(held_of[0], dec_ids)
    first_full = plane_full(held_of[0])
    ids_plane = spread(jnp.stack([dec_ids, targets]), "ctx")
    ids_all = spread(in_blocks(ids_plane[:, 0]), "fsdp").reshape(
        fsdp_count, ctx_count, tp_count, dec_rows
    )
    target_blocks = in_blocks(ids_plane[:, 1])

    ids_local = ids_all.transpose(2, 0, 1, 3).reshape(-1) - tp_index * vocab_local
    ids_inside = jnp.logical_and(ids_local >= 0, ids_local < vocab_local)
    looked = lookup(jnp.where(ids_inside, ids_local, 0), embed_table)
    looked = to_low(jnp.where(ids_inside[:, None], looked, 0.0))
    looked = looked.reshape(tp_count, fsdp_count * ctx_count * dec_rows, thick)
    looked = lax.psum_scatter(looked, "tp", scatter_dimension=0, tiled=False)
    looked = looked.reshape(fsdp_count * ctx_count, dec_rows, thick)
    looked = lax.all_to_all(looked, ("fsdp", "ctx"), 0, 0, tiled=True)
    embedded = looked.transpose(1, 0, 2).reshape(dec_rows, D).astype(jnp.float32)

    packed = jnp.concatenate(
        [
            teach_probs,
            teach_ids.astype(jnp.float32),
            teach_rows[..., None].astype(jnp.float32),
        ],
        axis=2,
    )
    packed, held_of[1] = together(packed, held_of[1])
    unpack(groups[1], plane_full(held_of[1]))
    packed = in_blocks(spread(packed, "ctx"))
    top_count = teach_probs.shape[2]
    taught = (
        packed[:, :, -1].astype(jnp.int32),
        packed[:, :, top_count : 2 * top_count].astype(jnp.int32),
        packed[:, :, :top_count],
    )
    token_total = clip_count * fsdp_count * dec_rows * ctx_count
    teach_total = clip_count * fsdp_count * teach_count * ctx_count
    token_share = 1.0 / token_total
    row_place = jnp.arange(dec_rows, dtype=jnp.int32)
    taught_rows = taught[0] - part_of_block[:, None] * dec_rows
    hits = taught_rows[:, :, None] == row_place[None, None, :]
    rank_taught = jnp.sum(
        jnp.where(hits, jnp.arange(teach_count, dtype=jnp.int32)[None, :, None], 0), axis=1
    )
    is_taught = jnp.any(hits, axis=1)
    earlier = row_place[None, :, None] < row_place[None, None, :]
    rank_other = teach_count + jnp.sum(
        jnp.where(jnp.logical_and(earlier, ~is_taught[:, :, None]), 1, 0), axis=1
    )
    new_place = jnp.where(is_taught, rank_taught, rank_other)
    moved = new_place[:, None, :] == row_place[None, :, None]
    vocab_start = tp_index * vocab_local + ctx_index * vocab_part
    vocab_valid = jnp.minimum(vocab_part, vocab_local - ctx_index * vocab_part)
    target_local = (
        jnp.sum(jnp.where(moved, target_blocks[:, None, :], 0), axis=2) - vocab_start
    )
    target_local = jnp.where(
        jnp.logical_and(target_local >= 0, target_local < vocab_valid), target_local, -1
    ).reshape(-1, 1)
    share_taught = taught[2] / teach_total
    row_weight = jnp.concatenate(
        [
            token_share + jnp.sum(share_taught, axis=2),
            jnp.full((blocks, dec_rows - teach_count), token_share, jnp.float32),
        ],
        axis=1,
    ).reshape(-1)
    taught_local = (taught[1] - vocab_start).reshape(blocks * teach_count, -1)
    inside = jnp.logical_and(taught_local >= 0, taught_local < vocab_valid)
    high = jnp.where(inside, taught_local // LANES, -1)
    low_part = taught_local - taught_local // LANES * LANES
    high_hot = jnp.where(
        high[:, None, :] == jnp.arange(vocab_part // LANES, dtype=jnp.int32)[None, :, None],
        share_taught.reshape(blocks * teach_count, 1, -1),
        0.0,
    ).astype(jnp.bfloat16)
    low_hot = (
        low_part[:, None, :] == jnp.arange(LANES, dtype=jnp.int32)[None, :, None]
    ).astype(jnp.bfloat16)
    teach_weight = to_low(product("rhk,rlk->hrl", high_hot, low_hot))
    mask_wide = jnp.pad(vocab_mask, (0, ctx_count * vocab_part - vocab_local))
    mask_part = lax.dynamic_slice_in_dim(mask_wide, ctx_index * vocab_part, vocab_part, 0)
    bias_row = jnp.where(mask_part > 0, 0.0, NEG_FILL).astype(jnp.float32)[None, :]

    if paired:
        partner_block = (1 - ctx_index) * tp_count + tp_index
        mine = pick(mel_frames, clip_index)
        arrived = lax.ppermute(pick(mel_frames, partner_block // 2), "ctx", [(0, 1), (1, 0)])
        clip_mel = jnp.where(
            ctx_index == 0,
            jnp.concatenate([mine, arrived], axis=0),
            jnp.concatenate([arrived, mine], axis=0),
        )
    else:
        clip_mel = lax.all_gather(pick(mel_frames, clip_index), "ctx", axis=0, tiled=True)
    frame_pairs = jnp.pad(clip_mel.reshape(-1, 2 * MEL), ((1, 1), (0, 0)))
    near = lax.dynamic_slice_in_dim(frame_pairs, part_index * enc_rows, enc_rows + 2, 0)
    evens, odds = near[:, :MEL], near[:, MEL:]
    evens, odds, held_of[2], held_of[3], table_held, first_full = together(
        evens, odds, held_of[2], held_of[3], table_held, first_full
    )
    rest_full = plane_full(jnp.concatenate(held_of[2:], axis=1))
    offset = 0
    for group, held in zip(groups[2:], held_of[2:]):
        unpack(group, rest_full[:, :, :, offset : offset + held.shape[1]])
        offset += held.shape[1]
    table_block = lax.all_gather(table_held, "fsdp", axis=0, tiled=True)
    conv_full = first_full[:, :, :, : KW * piece].transpose(2, 0, 1, 3, 4).reshape(KW, D, D)
    unpack(groups[0], first_full)
    taps_even = jnp.concatenate([odds[:-2], evens[1:-1], odds[1:-1]], axis=1)
    taps_odd = jnp.concatenate([evens[:-1], odds[:-1], evens[1:]], axis=1)

    hidden_bias = small_params[27:NVEC].reshape(2, FF)
    kernel_one = to_low(small_params[NVEC : NVEC + KW * MEL])
    pre_even = product("fm,mo->fo", taps_even, kernel_one) + small_params[14]
    pre_odd = product("fm,mo->fo", taps_odd, kernel_one) + small_params[14]
    odd_open = jnp.logical_or(
        part_index > 0, jnp.arange(enc_rows + 1, dtype=jnp.int32) > 0
    )[:, None]
    first_even = to_low(gelu_exact(pre_even))
    first_odd = to_low(jnp.where(odd_open, gelu_exact(pre_odd), 0.0))
    first_even, first_odd, teach_weight = together(first_even, first_odd, teach_weight)
    taps_two = (first_odd[:-1], first_even, first_odd[1:])
    second_pre = small_params[15]
    for tap in range(KW):
        second_pre = second_pre + product("ji,oi->jo", taps_two[tap], conv_full[tap])
    stream_zero = gelu_exact(second_pre) + sinusoid(part_index * enc_rows, enc_rows, D)
    enc_one = to_low(layer_norm(stream_zero, small_params[0], small_params[1]))
    enc_one_clip = spread_rows(enc_one)
    enc_weights = (narrow_full[0], narrow_full[1], narrow_full[2], narrow_full[9])
    attn_out, enc_saved = attention_forward(
        enc_one,
        enc_one_clip,
        enc_weights,
        (small_params[16], small_params[17], small_params[18]),
        None,
        None,
    )
    stream_one = stream_zero + attn_out
    enc_two = to_low(layer_norm(stream_one, small_params[2], small_params[3]))
    feed_out, enc_feed_saved = feed_forward_pass(
        enc_two, feed_full[0], hidden_bias[0], feed_full[1], small_params[19]
    )
    stream_two = stream_one + feed_out
    encoded = to_low(layer_norm(stream_two, small_params[4], small_params[5]))
    encoded_clip = spread_rows(encoded)

    dec_start = part_index * dec_rows
    query_place = dec_start + row_place
    if paired:
        key_place = jnp.concatenate([query_place, (1 - part_index) * dec_rows + row_place])
    else:
        key_place = jnp.arange(dec_rows * part_count, dtype=jnp.int32)
    position_start = NVEC + KW * MEL
    tokens_zero = embedded + lax.dynamic_slice_in_dim(
        small_params, position_start + dec_start, dec_rows, 0
    )
    dec_one = to_low(layer_norm(tokens_zero, small_params[6], small_params[7]))
    dec_one_clip = spread_rows(dec_one)
    self_weights = (narrow_full[3], narrow_full[4], narrow_full[5], narrow_full[10])
    self_out, self_saved = attention_forward(
        dec_one,
        dec_one_clip,
        self_weights,
        (small_params[20], small_params[21], small_params[22]),
        key_place,
        query_place,
    )
    tokens_one = tokens_zero + self_out
    dec_two = to_low(layer_norm(tokens_one, small_params[8], small_params[9]))
    cross_weights = (narrow_full[6], narrow_full[7], narrow_full[8], narrow_full[11])
    cross_out, cross_saved = attention_forward(
        dec_two,
        encoded_clip,
        cross_weights,
        (small_params[23], small_params[24], small_params[25]),
        None,
        None,
    )
    tokens_two = tokens_one + cross_out
    dec_three = to_low(layer_norm(tokens_two, small_params[10], small_params[11]))
    dec_feed_out, dec_feed_saved = feed_forward_pass(
        dec_three, feed_full[2], hidden_bias[1], feed_full[3], small_params[26]
    )
    tokens_three = tokens_two + dec_feed_out
    tokens_three, table_block = together(tokens_three, table_block)
    final = to_low(layer_norm(tokens_three, small_params[12], small_params[13]))

    moved_own = pick(moved, block_index).astype(jnp.bfloat16)
    final_moved = to_low(product("np,pd->nd", moved_own, final))
    final_all = lax.all_gather(final_moved, PLANE, axis=0, tiled=True)
    top_lanes, total_lanes, picked, dots = loss_stats(
        final_all, table_block, bias_row, target_local, teach_weight, blocks
    )
    top_own = jnp.max(top_lanes, axis=1)
    total_own = jnp.sum(total_lanes * jnp.exp(top_lanes - top_own[:, None]), axis=1)
    stats = lax.all_gather(jnp.stack([top_own, total_own]), PLANE, axis=0)
    joint_top = jnp.max(stats[:, 0], axis=0)
    joint_total = jnp.sum(stats[:, 1] * jnp.exp(stats[:, 0] - joint_top), axis=0)
    log_total = joint_top + jnp.log(joint_total)
    loss_term = (
        jnp.sum(row_weight * log_total) / blocks
        + jnp.sum(teach_probs * jnp.log(teach_probs)) / (teach_total * tp_count)
        - jnp.sum(picked) * token_share
        - jnp.sum(dots)
    )
    levels = (log_total - jnp.log(row_weight))[:, None]
    final_grad, table_grad = loss_grads(
        final_all, table_block, bias_row, target_local, levels, teach_weight, blocks, token_share
    )
    grad_final_moved = lax.psum_scatter(final_grad, PLANE, scatter_dimension=0, tiled=True)
    grad_final = product("np,nd->pd", moved_own, grad_final_moved)

    table_sum = lax.psum_scatter(table_grad, "fsdp", scatter_dimension=0, tiled=True)

    def cut_narrow(grad, height):
        return (
            to_low(grad)
            .reshape(fsdp_count, ctx_count, tp_count, height, D)
            .transpose(1, 2, 0, 3, 4)
        )

    def cut_feed(grad):
        return (
            to_low(grad)
            .reshape(fsdp_count, ctx_count, thick, tp_count, D)
            .transpose(1, 3, 0, 2, 4)
        )

    def packed_grads(pieces):
        held = jnp.concatenate(pieces, axis=3)
        return held.reshape((blocks,) + held.shape[2:])

    def plane_sum(held):
        return lax.psum_scatter(held, PLANE, scatter_dimension=0, tiled=False)

    def own_columns(grad, heights):
        cut = to_low(grad).reshape(grad.shape[0], tp_count, D // tp_count).swapaxes(0, 1)
        arrived = lax.all_to_all(cut, "tp", 0, 0, tiled=True).astype(jnp.float32)
        out, offset = [], 0
        for height in heights:
            out.append(
                arrived[:, offset : offset + height].reshape(
                    tp_count * height, D // tp_count
                )
            )
            offset += height
        return out

    row_grads = {}
    grad_three, row_grads[12], row_grads[13] = norm_back(
        tokens_three, small_params[12], small_params[13], grad_final
    )
    grad_feed = to_low(grad_three)
    row_grads[26] = jnp.sum(grad_feed, axis=0, dtype=jnp.float32)
    feed_grad_2, feed_grad_3, dec_bias_in, back = feed_backward(
        dec_three, feed_full[2], feed_full[3], dec_feed_saved, grad_feed
    )
    back, feed_grad_2, feed_grad_3 = together(back, to_low(feed_grad_2), to_low(feed_grad_3))
    back, row_grads[10], row_grads[11] = norm_back(
        tokens_two, small_params[10], small_params[11], back
    )
    grad_two = grad_three + back
    grad_cross = to_low(grad_two)
    row_grads[25] = jnp.sum(grad_cross, axis=0, dtype=jnp.float32)
    cross_grads, row_grads[23], row_grads[24], back_q, back_encoded = attention_backward(
        dec_two, encoded_clip, cross_weights, cross_saved, grad_cross, None, None
    )
    back, row_grads[8], row_grads[9] = norm_back(
        tokens_one, small_params[8], small_params[9], back_q
    )
    grad_one = grad_two + back
    grad_self = to_low(grad_one)
    row_grads[22] = jnp.sum(grad_self, axis=0, dtype=jnp.float32)
    self_grads, row_grads[20], row_grads[21], back_q, back_k = attention_backward(
        dec_one, dec_one_clip, self_weights, self_saved, grad_self, key_place, query_place
    )
    held_dec = packed_grads(
        [cut_narrow(grad, piece) for grad in self_grads + cross_grads]
        + [cut_feed(feed_grad_2), cut_feed(feed_grad_3)]
    )
    back, row_grads[6], row_grads[7] = norm_back(
        tokens_zero, small_params[6], small_params[7], back_q + collect_rows(back_k)
    )
    grad_zero = grad_one + back
    position_rows = lax.dynamic_update_slice_in_dim(
        jnp.zeros((dec_rows * part_count, D), jnp.float32), grad_zero, dec_start, 0
    )
    sent = to_low(grad_zero).reshape(dec_rows, fsdp_count * ctx_count, thick).swapaxes(0, 1)
    sent = lax.all_to_all(sent, ("fsdp", "ctx"), 0, 0, tiled=True)
    sent = sent.reshape(fsdp_count, ctx_count, dec_rows, thick)
    sent = lax.all_gather(sent, "tp", axis=0).reshape(-1, thick).astype(jnp.float32)
    embed_grad = scatter_add(jnp.where(ids_inside, ids_local, vocab_local), sent, vocab_local)

    back_encoded, held_dec = together(back_encoded, held_dec)
    part_dec = plane_sum(held_dec)
    back_encoded_own = collect_rows(back_encoded)
    grad_stream_two, row_grads[4], row_grads[5] = norm_back(
        stream_two, small_params[4], small_params[5], back_encoded_own
    )
    grad_feed = to_low(grad_stream_two)
    row_grads[19] = jnp.sum(grad_feed, axis=0, dtype=jnp.float32)
    feed_grad_0, feed_grad_1, enc_bias_in, back = feed_backward(
        enc_two, feed_full[0], feed_full[1], enc_feed_saved, grad_feed
    )
    back, row_grads[2], row_grads[3] = norm_back(
        stream_one, small_params[2], small_params[3], back
    )
    grad_stream_one = grad_stream_two + back
    grad_stream_one, feed_grad_0, feed_grad_1, table_sum = together(
        grad_stream_one, to_low(feed_grad_0), to_low(feed_grad_1), table_sum
    )
    grad_attn = to_low(grad_stream_one)
    row_grads[18] = jnp.sum(grad_attn, axis=0, dtype=jnp.float32)
    enc_grads, row_grads[16], row_grads[17], back_q, back_k = attention_backward(
        enc_one, enc_one_clip, enc_weights, enc_saved, grad_attn, None, None
    )
    back, row_grads[0], row_grads[1] = norm_back(
        stream_zero, small_params[0], small_params[1], back_q + collect_rows(back_k)
    )
    grad_stream_zero = grad_stream_one + back
    enc_cuts = [cut_narrow(grad, piece) for grad in enc_grads] + [
        cut_feed(feed_grad_0),
        cut_feed(feed_grad_1),
    ]
    grad_stream_zero, enc_cuts = together(grad_stream_zero, enc_cuts)
    sum_dec = sum_to_owner(part_dec, "fsdp")
    dec_list = own_columns(sum_dec[: 8 * piece], (piece,) * 8)
    table_sum = table_sum.reshape(ctx_count, thick, vocab_part)
    table_sum = in_order(
        sent_to_owners(lambda step: pick(table_sum, lax.rem(ctx_index + step, ctx_count)), "ctx"),
        "ctx",
    )
    table_sum = table_sum.swapaxes(0, 1).reshape(thick, ctx_count * vocab_part)[:, :vocab_local]
    grad_second = to_low(gelu_back(second_pre, grad_stream_zero))
    row_grads[15] = jnp.sum(grad_second, axis=0, dtype=jnp.float32)
    conv_grads = [product("jo,ji->oi", grad_second, taps_two[tap]) for tap in range(KW)]
    part_enc = plane_sum(
        packed_grads(
            enc_cuts + [cut_narrow(jnp.concatenate(conv_grads, axis=0), KW * piece)]
        )
    )
    grad_taps = [product("jo,oi->ji", grad_second, conv_full[tap]) for tap in range(KW)]
    grad_odd = jnp.pad(grad_taps[0], ((0, 1), (0, 0))) + jnp.pad(grad_taps[2], ((1, 0), (0, 0)))
    grad_pre_even = to_low(gelu_back(pre_even, grad_taps[1]))
    grad_pre_odd = to_low(jnp.where(odd_open, gelu_back(pre_odd, grad_odd), 0.0))
    row_grads[14] = jnp.sum(grad_pre_even, axis=0, dtype=jnp.float32) + jnp.sum(
        grad_pre_odd, axis=0, dtype=jnp.float32
    )
    kernel_rows = product("fm,fo->mo", taps_even, grad_pre_even) + product(
        "fm,fo->mo", taps_odd, grad_pre_odd
    )

    vector_rows = jnp.concatenate(
        [
            jnp.stack([row_grads[row] for row in range(27)]),
            enc_bias_in.reshape(4, D),
            dec_bias_in.reshape(4, D),
            kernel_rows,
        ]
    )
    small_rows = jnp.concatenate([vector_rows, position_rows])
    small_count = small_rows.shape[0]
    small_rows = jnp.pad(small_rows, ((0, -small_count % (8 * blocks)), (0, 0)))
    small_rows, part_enc, sum_dec, dec_list, table_sum, embed_grad = together(
        small_rows, part_enc, sum_dec, dec_list, table_sum, embed_grad
    )
    small_part = lax.psum_scatter(small_rows, PLANE, scatter_dimension=0, tiled=True)
    small_part = exchanged_sum(small_part, ("fsdp",))
    small_grad = lax.all_gather(small_part, PLANE, axis=0, tiled=True)[:small_count]
    sum_enc = sum_to_owner(part_enc, "fsdp")
    enc_feed_end = 4 * piece + 2 * thick
    enc_list = own_columns(
        jnp.concatenate([sum_enc[: 4 * piece], sum_enc[enc_feed_end:]]),
        (piece,) * 4 + (KW * piece,),
    )
    shard_conv = enc_list[4]

    shard_table = table_sum.astype(jnp.float32) + embed_grad
    shard_proj = jnp.stack(enc_list[0:3] + dec_list[0:3] + dec_list[4:7])
    shard_out = jnp.stack([enc_list[3], dec_list[3], dec_list[7]])
    shard_feed = jnp.concatenate([sum_enc[4 * piece : enc_feed_end], sum_dec[8 * piece :]])
    shard_feed = shard_feed.reshape(4, thick, D)
    local_squares = (
        jnp.sum(shard_proj * shard_proj)
        + jnp.sum(shard_out * shard_out)
        + jnp.sum(shard_feed * shard_feed)
        + jnp.sum(shard_conv * shard_conv)
        + jnp.sum(shard_table * shard_table)
        + jnp.sum(small_part * small_part) / fsdp_count
    )
    loss_value, squares = exchanged_sum(jnp.stack([loss_term, local_squares]), ALL)
    grad_norm = jnp.sqrt(squares)
    factor = jnp.minimum(1.0, CLIP_NORM / (grad_norm + 1e-06))
    results = [
        nesterov(projections, shard_proj, moment_projections, average_projections, factor),
        nesterov(out_proj, shard_out, moment_out_proj, average_out_proj, factor),
        nesterov(feed_forward, shard_feed, moment_feed_forward, average_feed_forward, factor),
        nesterov(conv_kernels, shard_conv, moment_conv_kernels, average_conv_kernels, factor),
        tuple(
            part.T
            for part in nesterov(
                embed_table.T, shard_table, moment_embed_table.T, average_embed_table.T, factor
            )
        ),
        nesterov(small_params, small_grad, moment_small_params, average_small_params, factor),
    ]
    return (loss_value, grad_norm) + tuple(
        result[kind] for kind in range(3) for result in results
    )


def solution(mesh):
    by_rows = P(None, ("fsdp", "ctx"), "tp")
    weights = (
        by_rows,
        by_rows,
        by_rows,
        P(("fsdp", "ctx"), "tp"),
        P("tp", ("fsdp", "ctx")),
        P(),
    )
    pair = P("fsdp", "ctx")
    wide = P("fsdp", "ctx", None)
    in_specs = (wide, pair, pair, pair, wide, wide, P("tp")) + 3 * weights
    out_specs = (P(), P()) + 3 * weights
    return jax.shard_map(local, mesh=mesh, in_specs=in_specs, out_specs=out_specs, check_vma=False)
```
